32 devices in a mesh: segment: 2 (over y), tile: 16 (over z, x, core).
Axes of the slice: x: 2, y: 2, z: 4, core: 2. Of those that a mesh axis runs over, the one named last changes fastest.
Arguments:
- coarse: bfloat16 [2, 8, 64, 128], P(None, None, 'tile'), may hold values from -6 to 6
- noise_draw: float32 [2, 4, 128, 128], P(None, None, 'tile'), may hold values from -6 to 6
- reg_in: bfloat16 [192, 72], replicated, may hold values from -0.75 to 0.75
- reg_mid: bfloat16 [2, 192, 1728], replicated, may hold values from -0.15625 to 0.15625
- reg_out: bfloat16 [4, 192], replicated, may hold values from -0.4375 to 0.4375
- diff_in: bfloat16 [256, 144], replicated, may hold values from -0.5 to 0.5
- diff_skip: bfloat16 [256, 192], replicated, may hold values from -0.4375 to 0.4375
- diff_mid: bfloat16 [256, 2304], replicated, may hold values from -0.125 to 0.125
- diff_out: bfloat16 [4, 256], replicated, may hold values from -0.375 to 0.375
- noise_embed: float32 [256], replicated, may hold values from -5 to 5
Outputs:
- fields: float32 [2, 2, 4, 64, 128], P('segment', None, None, 'tile')
The draws below stay inside these ranges and needn't reach their ends.
All inputs are finite; a program needn't handle non-finite values.
Results may differ from the reference program's by a relative error of at most 0.004.
Values may be sent and summed in bfloat16 or wider, within the bound.
No kernel may reach another device: no remote copies, remote signals or barrier semaphores. Data moves between devices by JAX's collectives and lax.ppermute only.
A program may use at most 64 MiB of HBM per device.

```python
import math
import jax
import jax.numpy as jnp
from jax import lax

CR = 192
CD = 256
GROUPS = 32
IN_F = 8
OUT_F = 4
REG_BLOCKS = 2
MARGIN = 2
TH = 4
NX = 128
MB = 2
PR = 8
NY = 64
NOISE_ROWS = 128
N_TILE = 16


def steps_of(key, shape, cuts, low, top_value):
    factor_of, own = 1.0, jax.random.fold_in(key, 6)
    for dim, blocks in cuts:
        heights = jnp.exp(jax.random.uniform(jax.random.fold_in(own, dim), (blocks,), jnp.float32, low / len(cuts), top_value / len(cuts)))
        factor_of = factor_of * jnp.repeat(heights, shape[dim] // blocks).reshape([-1 if axis == dim else 1 for axis in range(len(shape))])
    return factor_of


def gaussian(own_key, extent, deviation, limit, shards=(), held_as=jnp.bfloat16):
    values = jax.random.normal(own_key, extent, jnp.float32) * deviation
    if len(shards) > 0:
        values = steps_of(own_key, extent, shards, -0.22, 0.18) * values
    return jnp.clip(values, min=-limit, max=limit).astype(held_as)


def setup_inputs(seed: int = 0) -> dict:
    key_of = jax.random.split(jax.random.key(seed), 11)
    return {
        "coarse": gaussian(key_of[0], (MB, IN_F, NY, NX), 1.0, 6.0, ((2, 16),)),
        "noise_draw": gaussian(key_of[1], (MB, OUT_F, NOISE_ROWS, NX), 1.0, 6.0, ((2, 16),), jnp.float32),
        "reg_in": gaussian(key_of[2], (CR, 9 * IN_F), (9 * IN_F) ** -0.5, 0.75),
        "reg_mid": gaussian(key_of[3], (REG_BLOCKS, CR, 9 * CR), (9 * CR) ** -0.5, 0.15625),
        "reg_out": gaussian(key_of[4], (OUT_F, CR), CR ** -0.5, 0.4375),
        "diff_in": gaussian(key_of[5], (CD, 9 * (2 * OUT_F + IN_F)), (9 * (2 * OUT_F + IN_F)) ** -0.5, 0.5),
        "diff_skip": gaussian(key_of[6], (CD, CR), CR ** -0.5, 0.4375),
        "diff_mid": gaussian(key_of[7], (CD, 9 * CD), (9 * CD) ** -0.5, 0.125),
        "diff_out": gaussian(key_of[8], (OUT_F, CD), CD ** -0.5, 0.375),
        "noise_embed": gaussian(key_of[9], (CD,), 1.0, 5.0, (), jnp.float32),
    }


sigma_high = 4.0
sigma_low = 0.5
sigma_data = 0.5

def conv_three(weight, grid_rows):
    channels = grid_rows.shape[0]
    row_count = grid_rows.shape[1]
    col_count = grid_rows.shape[2]
    padded = jnp.pad(grid_rows, ((0, 0), (1, 1), (1, 1)))
    stacked = jnp.concatenate([padded[:, shift_row:shift_row + row_count, shift_col:shift_col + col_count] for shift_row in range(3) for shift_col in range(3)], axis=0)
    flattened = stacked.reshape(9 * channels, row_count * col_count)
    result = jnp.dot(weight.astype(jnp.float32), flattened.astype(jnp.float32))
    return result.reshape(weight.shape[0], row_count, col_count)

def point_map(weight, grid_rows):
    channels = grid_rows.shape[0]
    flattened = grid_rows.reshape(channels, grid_rows.shape[1] * grid_rows.shape[2])
    result = jnp.dot(weight.astype(jnp.float32), flattened.astype(jnp.float32))
    return result.reshape(weight.shape[0], grid_rows.shape[1], grid_rows.shape[2])

def group_norm(hidden):
    grouped = hidden.reshape(GROUPS, -1)
    centre = grouped - lax.optimization_barrier(jnp.mean(grouped, axis=1, keepdims=True))
    variance = lax.optimization_barrier(jnp.mean(centre * centre, axis=1, keepdims=True))
    return (centre * lax.rsqrt(variance + 1e-05)).reshape(hidden.shape)

def activate(hidden):
    return jax.nn.silu(group_norm(hidden)).astype(jnp.bfloat16)

def regression(coarse_patch, reg_in, reg_mid, reg_out):
    hidden = conv_three(reg_in, coarse_patch)
    for block_index in range(reg_mid.shape[0]):
        hidden = hidden + conv_three(reg_mid[block_index], activate(hidden))
    return (point_map(reg_out, activate(hidden)), hidden)

def diffusion(coarse_patch, mean_patch, skip_patch, noise_patch, diff_in, diff_skip, diff_mid, diff_out, noise_embed):
    skip_term = point_map(diff_skip, skip_patch)

    def denoise(current, sigma_now):
        total_var = sigma_now * sigma_now + sigma_data * sigma_data
        input_scale = 1.0 / math.sqrt(total_var)
        skip_coef = sigma_data * sigma_data / total_var
        out_coef = sigma_now * sigma_data / math.sqrt(total_var)
        model_in = jnp.concatenate([(input_scale * current).astype(jnp.bfloat16), coarse_patch, mean_patch], axis=0)
        hidden = conv_three(diff_in, model_in) + skip_term + math.log(sigma_now) / 4.0 * noise_embed[:, None, None]
        hidden = hidden + conv_three(diff_mid, activate(hidden))
        return skip_coef * current + out_coef * point_map(diff_out, activate(hidden))
    initial = sigma_high * noise_patch
    denoised = denoise(initial, sigma_high)
    stepped = initial + (sigma_low - sigma_high) * (initial - denoised) / sigma_high
    return denoise(stepped, sigma_low)

def intersection_average(patches):
    summed = patches[:, :, MARGIN:MARGIN + TH]
    summed = summed.at[1:, :, :MARGIN].add(patches[:-1, :, MARGIN + TH:])
    summed = summed.at[:-1, :, TH - MARGIN:].add(patches[1:, :, :MARGIN])
    row_ids = jnp.arange(TH, dtype=jnp.int32)
    tile_pos = jnp.arange(N_TILE, dtype=jnp.int32)
    above = jnp.logical_and(tile_pos[:, None] > 0, row_ids[None, :] < MARGIN)
    below = jnp.logical_and(tile_pos[:, None] < N_TILE - 1, row_ids[None, :] >= TH - MARGIN)
    cover_count = 1.0 + above.astype(jnp.float32) + below.astype(jnp.float32)
    averaged = summed / cover_count[:, None, :, None]
    return jnp.transpose(averaged, (1, 0, 2, 3)).reshape(patches.shape[1], NY, NX)

def reference(coarse, noise_draw, reg_in, reg_mid, reg_out, diff_in, diff_skip, diff_mid, diff_out, noise_embed):
    tile_ids = jnp.arange(N_TILE, dtype=jnp.int32)
    mean_list = []
    final_list = []
    for sample in range(MB):
        coarse_grid = jnp.pad(coarse[sample], ((0, 0), (MARGIN, MARGIN), (0, 0)))

        def reg_patch(tile_now):
            coarse_patch = lax.dynamic_slice_in_dim(coarse_grid, tile_now * TH, PR, 1)
            patch_out, hidden = regression(coarse_patch, reg_in, reg_mid, reg_out)
            return (patch_out, hidden[:, MARGIN:MARGIN + TH].astype(jnp.bfloat16))
        patch_outs, centres = lax.map(reg_patch, tile_ids)
        mean_band = intersection_average(patch_outs)
        mean_low = mean_band.astype(jnp.bfloat16)
        skip_grid = jnp.transpose(centres, (1, 0, 2, 3)).reshape(CR, NY, NX)
        condition = jnp.pad(jnp.concatenate([skip_grid, mean_low], axis=0), ((0, 0), (MARGIN, MARGIN), (0, 0)))

        def diff_patch(tile_now):
            coarse_patch = lax.dynamic_slice_in_dim(coarse_grid, tile_now * TH, PR, 1)
            cond_patch = lax.dynamic_slice_in_dim(condition, tile_now * TH, PR, 1)
            noise_patch = lax.dynamic_slice_in_dim(noise_draw[sample], tile_now * PR, PR, 1)
            return diffusion(coarse_patch, cond_patch[CR:], cond_patch[:CR], noise_patch, diff_in, diff_skip, diff_mid, diff_out, noise_embed)
        residual = lax.map(diff_patch, tile_ids)
        final_band = mean_low.astype(jnp.float32) + intersection_average(residual)
        mean_list.append(mean_band)
        final_list.append(final_band)
    return jnp.stack([jnp.stack(mean_list), jnp.stack(final_list)])
```

```python
import math

import jax
import jax.numpy as jnp
from jax import lax
from jax.experimental import pallas as pl
from jax.experimental.pallas import tpu as pltpu
from jax.sharding import PartitionSpec as P

GROUPS = 32
LANES = 128
BAND = 4
MARGIN = 2
ROWS = BAND + 2 * MARGIN

sigma_high = 4.0
sigma_low = 0.5
sigma_data = 0.5

F32 = jnp.float32
BF16 = jnp.bfloat16


def lanes(first, count=1):
    return slice(first * LANES, (first + count) * LANES)


def lane_ids(shape):
    return lax.broadcasted_iota(jnp.int32, shape, len(shape) - 1)


def col_shifts(chunk):
    lane = lane_ids(chunk.shape)
    zero = jnp.zeros_like(chunk)
    before = jnp.where(lane == 0, zero, pltpu.roll(chunk, 1, 1))
    after = jnp.where(lane == LANES - 1, zero, pltpu.roll(chunk, LANES - 1, 1))
    return before, chunk, after


def store_row(taps_ref, row, chunk):
    channels = chunk.shape[0]
    for b, piece in enumerate(col_shifts(chunk)):
        taps_ref[b * channels : (b + 1) * channels, lanes(row + 1)] = piece.astype(BF16)


def clear_edges(taps_ref):
    zero = jnp.zeros((taps_ref.shape[0], LANES), BF16)
    taps_ref[:, lanes(0)] = zero
    taps_ref[:, lanes(ROWS + 1)] = zero


def group_total(part):
    channels = part.shape[0]
    size = channels // GROUPS
    if size == 8:
        total = jnp.sum(part.reshape(GROUPS, 8, LANES), axis=(1, 2), keepdims=True)
        return jnp.broadcast_to(total, (GROUPS, 8, LANES)).reshape(channels, LANES)
    blocks = channels // 24
    tiles = part.reshape(blocks, 3, 8, LANES)
    row = lax.broadcasted_iota(jnp.int32, (blocks, 8, LANES), 1)
    v0, v1, v2 = tiles[:, 0], tiles[:, 1], tiles[:, 2]
    zero = jnp.zeros_like(v0)
    sums = (
        jnp.where(row < 6, v0, zero),
        jnp.where(row >= 6, v0, zero) + jnp.where(row < 4, v1, zero),
        jnp.where(row >= 4, v1, zero) + jnp.where(row < 2, v2, zero),
        jnp.where(row >= 2, v2, zero),
    )
    t0, t1, t2, t3 = (
        jnp.broadcast_to(jnp.sum(s, axis=(1, 2), keepdims=True), (blocks, 8, LANES)) for s in sums
    )
    m0 = jnp.where(row < 6, t0, t1)
    m1 = jnp.where(row < 4, t1, t2)
    m2 = jnp.where(row < 2, t2, t3)
    return jnp.stack([m0, m1, m2], axis=1).reshape(channels, LANES)


def norm_scales(hidden_ref):
    channels = hidden_ref.shape[0]
    share = 1.0 / (channels // GROUPS * ROWS * LANES)
    total = hidden_ref[:, lanes(0)]
    for r in range(1, ROWS):
        total = total + hidden_ref[:, lanes(r)]
    centre = group_total(total) * share
    square = jnp.zeros_like(centre)
    for r in range(ROWS):
        away = hidden_ref[:, lanes(r)] - centre
        square = square + away * away
    half = 0.5 * lax.rsqrt(group_total(square) * share + 1e-5)
    return centre, half


def act_row(hidden_ref, row, scales):
    centre, half = scales
    v = (hidden_ref[:, lanes(row)] - centre) * half
    return v + v * jnp.tanh(v)


def conv_rows(weight, taps_ref, first, count):
    depth = taps_ref.shape[0]
    out = None
    for a in range(3):
        term = jnp.dot(
            weight(a * depth, depth), taps_ref[:, lanes(first + a, count)], preferred_element_type=F32
        )
        out = term if out is None else out + term
    return out


def input_taps(rows, out_ref):
    shifted = [col_shifts(row) for row in rows]
    blank = jnp.zeros_like(rows[0])
    for i in range(ROWS):
        pieces = []
        for a in range(3):
            pieces.extend(shifted[i + a - 1] if 0 <= i + a - 1 < ROWS else [blank] * 3)
        out_ref[:, lanes(i)] = jnp.concatenate(pieces, axis=0).astype(BF16)


def place():
    tile = lax.axis_index("tile")
    count = lax.axis_size("tile")
    return lax.rem(tile, 2) == 0, tile == 0, tile == count - 1


def regress_kernel(
    coarse_ref, pair_ref, next_ref, far_ref, reg_in_ref, reg_mid_ref, reg_out_ref,
    skip_ref, reg_ref, send_skip_ref, send_reg_ref, outer_skip_ref, outer_reg_ref,
    taps_in, hidden_a, hidden_b, taps_a, taps_b,
):
    even, first, last = place()
    sample = lax.axis_index("segment")

    def rows_of(ref):
        block = ref[sample].astype(F32)
        return [block[:, r, :] for r in range(BAND)]

    own, pair, across, far = (rows_of(ref) for ref in (coarse_ref, pair_ref, next_ref, far_ref))
    window = [jnp.where(even, far[2 + i], pair[2 + i]) for i in range(2)]
    window += [jnp.where(even, across[i], own[i]) for i in range(4)]
    window += [jnp.where(even, own[i], across[i]) for i in range(4)]
    window += [jnp.where(even, pair[i], far[i]) for i in range(2)]
    no_low = jnp.logical_and(even, first)
    no_high = jnp.logical_and(jnp.logical_not(even), last)
    window = [
        jnp.where(no_low if i < 6 else no_high, jnp.zeros_like(w), w) for i, w in enumerate(window)
    ]
    rows_a = [jnp.where(even, window[i + 4], window[i]) for i in range(ROWS)]
    rows_b = [jnp.where(even, window[i], window[i + 4]) for i in range(ROWS)]
    for rows, hidden, taps in ((rows_a, hidden_a, taps_a), (rows_b, hidden_b, taps_b)):
        clear_edges(taps)
        input_taps(rows, taps_in)
        hidden[...] = jnp.dot(reg_in_ref[...], taps_in[...], preferred_element_type=F32)

    step = 2
    for block in range(reg_mid_ref.shape[0]):
        for hidden, taps in ((hidden_a, taps_a), (hidden_b, taps_b)):
            scales = norm_scales(hidden)
            for r in range(ROWS):
                store_row(taps, r, act_row(hidden, r, scales))
            for r in range(0, ROWS, step):
                hidden[:, lanes(r, step)] += conv_rows(
                    lambda at, depth: reg_mid_ref[block, :, at : at + depth], taps, r, step
                )

    scales = norm_scales(hidden_a)
    for r in range(ROWS):
        act = act_row(hidden_a, r, scales).astype(BF16)
        reg_ref[:, lanes(r)] = jnp.dot(reg_out_ref[...], act, preferred_element_type=F32)
    for i in range(BAND):
        skip_ref[:, lanes(i)] = hidden_a[:, lanes(MARGIN + i)].astype(BF16)
        send_reg_ref[:, lanes(i)] = jnp.where(even, reg_ref[:, lanes(4 + i)], reg_ref[:, lanes(i)])
    for i in range(MARGIN):
        send_skip_ref[:, lanes(i)] = jnp.where(
            even, hidden_a[:, lanes(4 + i)], hidden_a[:, lanes(2 + i)]
        ).astype(BF16)
        outer_skip_ref[:, lanes(i)] = jnp.where(
            even, hidden_b[:, lanes(4 + i)], hidden_b[:, lanes(2 + i)]
        ).astype(BF16)
    centre, half = norm_scales(hidden_b)
    for i in range(BAND):
        v = (jnp.where(even, hidden_b[:, lanes(4 + i)], hidden_b[:, lanes(i)]) - centre) * half
        act = (v + v * jnp.tanh(v)).astype(BF16)
        outer_reg_ref[:, lanes(i)] = jnp.dot(reg_out_ref[...], act, preferred_element_type=F32)


def denoise_kernel(
    coarse_ref, pair_ref, next_ref, noise_ref, skip_ref, reg_ref, pair_skip_ref, pair_reg_ref,
    outer_skip_ref, outer_reg_ref, diff_in_ref, diff_skip_ref, diff_mid_ref, diff_out_ref, embed_ref,
    mean_ref, band_ref, send_pair_ref, send_next_ref,
    taps_in, skips, base, hidden, taps,
):
    even, first, last = place()
    sample = lax.axis_index("segment")
    clear_edges(taps)

    def rows_of(ref):
        block = ref[sample].astype(F32)
        return [block[:, r, :] for r in range(block.shape[1])]

    own, pair, across = (rows_of(ref) for ref in (coarse_ref, pair_ref, next_ref))
    coarse = [jnp.where(even, across[2 + i], pair[2 + i]) for i in range(2)]
    coarse += own
    coarse += [jnp.where(even, pair[i], across[i]) for i in range(2)]
    reg = [reg_ref[:, lanes(r)] for r in range(ROWS)]
    up = [jnp.where(even, outer_reg_ref[:, lanes(i)], pair_reg_ref[:, lanes(i)]) for i in range(4)]
    down = [jnp.where(even, pair_reg_ref[:, lanes(i)], outer_reg_ref[:, lanes(i)]) for i in range(4)]
    mean = []
    for r in range(ROWS):
        both = 0.5 * (reg[r] + (up[r] if r < 4 else down[r - 4]))
        if r < MARGIN:
            mean.append(jnp.where(first, jnp.zeros_like(both), both))
        elif r < 4:
            mean.append(jnp.where(first, reg[r], both))
        elif r < MARGIN + BAND:
            mean.append(jnp.where(last, reg[r], both))
        else:
            mean.append(jnp.where(last, jnp.zeros_like(both), both))
    for i in range(BAND):
        mean_ref[:, lanes(i)] = mean[MARGIN + i]
    mean = [m.astype(BF16).astype(F32) for m in mean]
    for i in range(2):
        coarse[i] = jnp.where(first, jnp.zeros_like(coarse[i]), coarse[i])
        coarse[6 + i] = jnp.where(last, jnp.zeros_like(coarse[i]), coarse[6 + i])
        low = jnp.where(even, outer_skip_ref[:, lanes(i)], pair_skip_ref[:, lanes(i)])
        high = jnp.where(even, pair_skip_ref[:, lanes(i)], outer_skip_ref[:, lanes(i)])
        skips[:, lanes(i)] = jnp.where(first, jnp.zeros_like(low), low)
        skips[:, lanes(6 + i)] = jnp.where(last, jnp.zeros_like(high), high)
    skips[:, lanes(MARGIN, BAND)] = skip_ref[...]
    base[...] = jnp.dot(diff_skip_ref[...], skips[...], preferred_element_type=F32)

    channels = diff_mid_ref.shape[0]
    embed = jnp.broadcast_to(embed_ref[...], (LANES, channels)).T
    noise = rows_of(noise_ref)
    initial = [sigma_high * n for n in noise]
    step = 2

    def denoise(current, sigma_now):
        total_var = sigma_now * sigma_now + sigma_data * sigma_data
        input_scale = 1.0 / math.sqrt(total_var)
        skip_coef = sigma_data * sigma_data / total_var
        out_coef = sigma_now * sigma_data / math.sqrt(total_var)
        input_taps(
            [
                jnp.concatenate([input_scale * current[r], coarse[r], mean[r]], axis=0)
                for r in range(ROWS)
            ],
            taps_in,
        )
        shift = (math.log(sigma_now) / 4.0) * embed
        for r in range(0, ROWS, step):
            hidden[:, lanes(r, step)] = (
                jnp.dot(diff_in_ref[...], taps_in[:, lanes(r, step)], preferred_element_type=F32)
                + base[:, lanes(r, step)]
                + jnp.concatenate([shift] * step, axis=1)
            )
        scales = norm_scales(hidden)
        for r in range(ROWS):
            store_row(taps, r, act_row(hidden, r, scales))
        for r in range(0, ROWS, step):
            hidden[:, lanes(r, step)] += conv_rows(
                lambda at, depth: diff_mid_ref[:, at : at + depth], taps, r, step
            )
        scales = norm_scales(hidden)
        result = []
        for r in range(ROWS):
            act = act_row(hidden, r, scales).astype(BF16)
            out = jnp.dot(diff_out_ref[...], act, preferred_element_type=F32)
            result.append(skip_coef * current[r] + out_coef * out)
        return result

    denoised = denoise(initial, sigma_high)
    stepped = [
        x + (sigma_low - sigma_high) * (x - d) / sigma_high for x, d in zip(initial, denoised)
    ]
    final = denoise(stepped, sigma_low)
    for i in range(BAND):
        band_ref[:, lanes(i)] = final[MARGIN + i]
    for i in range(MARGIN):
        send_pair_ref[:, lanes(i)] = jnp.where(even, final[6 + i], final[i])
        send_next_ref[:, lanes(i)] = jnp.where(even, final[i], final[6 + i])


def average_kernel(mean_ref, band_ref, pair_ref, next_ref, own_ref, send_ref):
    even, first, last = place()
    lower = lax.axis_index("segment") == 0
    for i in range(BAND):
        here = band_ref[:, lanes(i)]
        mean = mean_ref[:, lanes(i)]
        j = i % MARGIN
        if i < MARGIN:
            other = jnp.where(even, next_ref[:, lanes(j)], pair_ref[:, lanes(j)])
            alone = first
        else:
            other = jnp.where(even, pair_ref[:, lanes(j)], next_ref[:, lanes(j)])
            alone = last
        value = jnp.where(alone, here, 0.5 * (here + other)) + mean.astype(BF16).astype(F32)
        own_ref[:, i, :] = jnp.where(lower, mean, value)
        send_ref[:, i, :] = jnp.where(lower, value, mean)


def output_kernel(own_ref, got_ref, out_ref):
    lower = lax.axis_index("segment") == 0
    own, got = own_ref[...], got_ref[...]
    out_ref[0, 0] = jnp.where(lower, own, got)
    out_ref[0, 1] = jnp.where(lower, got, own)


def call(kernel, name, outs, scratch=()):
    return pl.pallas_call(
        kernel,
        name=name,
        out_shape=[jax.ShapeDtypeStruct(shape, dtype) for shape, dtype in outs],
        scratch_shapes=[pltpu.VMEM(shape, dtype) for shape, dtype in scratch],
        compiler_params=pltpu.CompilerParams(vmem_limit_bytes=32 * 1024 * 1024),
    )


def shards(
    coarse, noise_draw, reg_in, reg_mid, reg_out, diff_in, diff_skip, diff_mid, diff_out, noise_embed
):
    tiles = lax.axis_size("tile")
    pairs = [(i, i ^ 1) for i in range(tiles)]
    nexts = [(i, (i - 1 if i % 2 == 0 else i + 1) % tiles) for i in range(tiles)]
    fars = [(i, (i + 2 if i % 2 == 0 else i - 2) % tiles) for i in range(tiles)]
    swap = [(0, 1), (1, 0)]
    width_r, width_d, fields = reg_in.shape[0], diff_in.shape[0], reg_out.shape[0]
    cells = ROWS * LANES

    pair_coarse = lax.ppermute(coarse, "tile", pairs)
    next_coarse = lax.ppermute(coarse, "tile", nexts)
    far_coarse = lax.ppermute(coarse, "tile", fars)
    skip, reg, send_skip, send_reg, outer_skip, outer_reg = call(
        regress_kernel,
        "regress",
        [
            ((width_r, BAND * LANES), BF16),
            ((fields, cells), F32),
            ((width_r, MARGIN * LANES), BF16),
            ((fields, BAND * LANES), F32),
            ((width_r, MARGIN * LANES), BF16),
            ((fields, BAND * LANES), F32),
        ],
        [
            ((reg_in.shape[1], cells), BF16),
            ((width_r, cells), F32),
            ((width_r, cells), F32),
            ((3 * width_r, cells + 2 * LANES), BF16),
            ((3 * width_r, cells + 2 * LANES), BF16),
        ],
    )(coarse, pair_coarse, next_coarse, far_coarse, reg_in, reg_mid, reg_out)
    pair_skip = lax.ppermute(send_skip, "tile", pairs)
    pair_reg = lax.ppermute(send_reg, "tile", pairs)
    mean, band, send_pair, send_next = call(
        denoise_kernel,
        "denoise",
        [
            ((fields, BAND * LANES), F32),
            ((fields, BAND * LANES), F32),
            ((fields, MARGIN * LANES), F32),
            ((fields, MARGIN * LANES), F32),
        ],
        [
            ((diff_in.shape[1], cells), BF16),
            ((width_r, cells), BF16),
            ((width_d, cells), F32),
            ((width_d, cells), F32),
            ((3 * width_d, cells + 2 * LANES), BF16),
        ],
    )(
        coarse, pair_coarse, next_coarse, noise_draw, skip, reg, pair_skip, pair_reg,
        outer_skip, outer_reg, diff_in, diff_skip, diff_mid, diff_out, noise_embed[None],
    )
    pair_band = lax.ppermute(send_pair, "tile", pairs)
    next_band = lax.ppermute(send_next, "tile", nexts)
    piece = ((fields, BAND, LANES), F32)
    own, send = call(average_kernel, "average", [piece, piece])(mean, band, pair_band, next_band)
    got = lax.ppermute(send, "segment", swap)
    (out,) = call(output_kernel, "output", [((1, 2, fields, BAND, LANES), F32)])(own, got)
    return out


def solution(mesh):
    return jax.shard_map(
        shards,
        mesh=mesh,
        in_specs=(P(None, None, "tile", None), P(None, None, "tile", None)) + (P(),) * 8,
        out_specs=P("segment", None, None, "tile", None),
        check_vma=False,
    )
```

```python
import math

import jax
import jax.numpy as jnp
from jax import lax
from jax.experimental import pallas as pl
from jax.experimental.pallas import tpu as pltpu
from jax.sharding import PartitionSpec as P

GROUPS = 32
LANES = 128
BAND = 4
MARGIN = 2
ROWS = BAND + 2 * MARGIN

sigma_high = 4.0
sigma_low = 0.5
sigma_data = 0.5

F32 = jnp.float32
BF16 = jnp.bfloat16


def lanes(first, count=1):
    return slice(first * LANES, (first + count) * LANES)


def lane_ids(shape):
    return lax.broadcasted_iota(jnp.int32, shape, len(shape) - 1)


def col_shifts(chunk):
    lane = lane_ids(chunk.shape)
    zero = jnp.zeros_like(chunk)
    before = jnp.where(lane == 0, zero, pltpu.roll(chunk, 1, 1))
    after = jnp.where(lane == LANES - 1, zero, pltpu.roll(chunk, LANES - 1, 1))
    return before, chunk, after


def store_row(taps_ref, row, chunk):
    channels = chunk.shape[0]
    for b, piece in enumerate(col_shifts(chunk)):
        taps_ref[b * channels : (b + 1) * channels, lanes(row + 1)] = piece.astype(BF16)


def clear_edges(taps_ref):
    zero = jnp.zeros((taps_ref.shape[0], LANES), BF16)
    taps_ref[:, lanes(0)] = zero
    taps_ref[:, lanes(ROWS + 1)] = zero


def group_total(part):
    channels = part.shape[0]
    size = channels // GROUPS
    if size == 8:
        total = jnp.sum(part.reshape(GROUPS, 8, LANES), axis=(1, 2), keepdims=True)
        return jnp.broadcast_to(total, (GROUPS, 8, LANES)).reshape(channels, LANES)
    blocks = channels // 24
    tiles = part.reshape(blocks, 3, 8, LANES)
    row = lax.broadcasted_iota(jnp.int32, (blocks, 8, LANES), 1)
    v0, v1, v2 = tiles[:, 0], tiles[:, 1], tiles[:, 2]
    zero = jnp.zeros_like(v0)
    sums = (
        jnp.where(row < 6, v0, zero),
        jnp.where(row >= 6, v0, zero) + jnp.where(row < 4, v1, zero),
        jnp.where(row >= 4, v1, zero) + jnp.where(row < 2, v2, zero),
        jnp.where(row >= 2, v2, zero),
    )
    t0, t1, t2, t3 = (
        jnp.broadcast_to(jnp.sum(s, axis=(1, 2), keepdims=True), (blocks, 8, LANES)) for s in sums
    )
    m0 = jnp.where(row < 6, t0, t1)
    m1 = jnp.where(row < 4, t1, t2)
    m2 = jnp.where(row < 2, t2, t3)
    return jnp.stack([m0, m1, m2], axis=1).reshape(channels, LANES)


def norm_scales(hidden_ref):
    channels = hidden_ref.shape[0]
    share = 1.0 / (channels // GROUPS * ROWS * LANES)
    total = hidden_ref[:, lanes(0)]
    for r in range(1, ROWS):
        total = total + hidden_ref[:, lanes(r)]
    centre = group_total(total) * share
    square = jnp.zeros_like(centre)
    for r in range(ROWS):
        away = hidden_ref[:, lanes(r)] - centre
        square = square + away * away
    half = 0.5 * lax.rsqrt(group_total(square) * share + 1e-5)
    return centre, half


def act_row(hidden_ref, row, scales):
    centre, half = scales
    v = (hidden_ref[:, lanes(row)] - centre) * half
    return v + v * jnp.tanh(v)


def conv_rows(weight, taps_ref, first, count):
    depth = taps_ref.shape[0]
    out = None
    for a in range(3):
        term = jnp.dot(
            weight(a * depth, depth), taps_ref[:, lanes(first + a, count)], preferred_element_type=F32
        )
        out = term if out is None else out + term
    return out


def input_taps(rows, out_ref):
    shifted = [col_shifts(row) for row in rows]
    blank = jnp.zeros_like(rows[0])
    for i in range(ROWS):
        pieces = []
        for a in range(3):
            pieces.extend(shifted[i + a - 1] if 0 <= i + a - 1 < ROWS else [blank] * 3)
        out_ref[:, lanes(i)] = jnp.concatenate(pieces, axis=0).astype(BF16)


def place():
    tile = lax.axis_index("tile")
    count = lax.axis_size("tile")
    return lax.rem(tile, 2) == 0, tile == 0, tile == count - 1


def prepare_kernel(coarse_ref, noise_ref, own_ref, initial_ref):
    sample = lax.axis_index("segment")
    block = coarse_ref[sample].astype(F32)
    for r in range(BAND):
        own_ref[:, lanes(r)] = block[:, r, :]
    block = noise_ref[sample]
    for r in range(ROWS):
        initial_ref[:, lanes(r)] = sigma_high * block[:, r, :]


def regress_kernel(
    own_ref, pair_ref, next_ref, far_ref, reg_in_ref, reg_mid_ref, reg_out_ref,
    skip_ref, reg_ref, send_skip_ref, send_reg_ref, outer_skip_ref, outer_reg_ref,
    taps_in, hidden_a, hidden_b, taps_a, taps_b,
):
    even, first, last = place()
    sample = lax.axis_index("segment")

    def rows_of(ref):
        block = ref[sample].astype(F32)
        return [block[:, r, :] for r in range(BAND)]

    own = [own_ref[:, lanes(r)] for r in range(BAND)]
    pair, across, far = (rows_of(ref) for ref in (pair_ref, next_ref, far_ref))
    window = [jnp.where(even, far[2 + i], pair[2 + i]) for i in range(2)]
    window += [jnp.where(even, across[i], own[i]) for i in range(4)]
    window += [jnp.where(even, own[i], across[i]) for i in range(4)]
    window += [jnp.where(even, pair[i], far[i]) for i in range(2)]
    no_low = jnp.logical_and(even, first)
    no_high = jnp.logical_and(jnp.logical_not(even), last)
    window = [
        jnp.where(no_low if i < 6 else no_high, jnp.zeros_like(w), w) for i, w in enumerate(window)
    ]
    rows_a = [jnp.where(even, window[i + 4], window[i]) for i in range(ROWS)]
    rows_b = [jnp.where(even, window[i], window[i + 4]) for i in range(ROWS)]
    for rows, hidden, taps in ((rows_a, hidden_a, taps_a), (rows_b, hidden_b, taps_b)):
        clear_edges(taps)
        input_taps(rows, taps_in)
        hidden[...] = jnp.dot(reg_in_ref[...], taps_in[...], preferred_element_type=F32)

    step = 2
    for block in range(reg_mid_ref.shape[0]):
        for hidden, taps in ((hidden_a, taps_a), (hidden_b, taps_b)):
            scales = norm_scales(hidden)
            for r in range(ROWS):
                store_row(taps, r, act_row(hidden, r, scales))
            for r in range(0, ROWS, step):
                hidden[:, lanes(r, step)] += conv_rows(
                    lambda at, depth: reg_mid_ref[block, :, at : at + depth], taps, r, step
                )

    scales = norm_scales(hidden_a)
    for r in range(ROWS):
        act = act_row(hidden_a, r, scales).astype(BF16)
        reg_ref[:, lanes(r)] = jnp.dot(reg_out_ref[...], act, preferred_element_type=F32)
    for i in range(BAND):
        skip_ref[:, lanes(i)] = hidden_a[:, lanes(MARGIN + i)].astype(BF16)
        send_reg_ref[:, lanes(i)] = jnp.where(even, reg_ref[:, lanes(4 + i)], reg_ref[:, lanes(i)])
    for i in range(MARGIN):
        send_skip_ref[:, lanes(i)] = jnp.where(
            even, hidden_a[:, lanes(4 + i)], hidden_a[:, lanes(2 + i)]
        ).astype(BF16)
        outer_skip_ref[:, lanes(i)] = jnp.where(
            even, hidden_b[:, lanes(4 + i)], hidden_b[:, lanes(2 + i)]
        ).astype(BF16)
    centre, half = norm_scales(hidden_b)
    for i in range(BAND):
        v = (jnp.where(even, hidden_b[:, lanes(4 + i)], hidden_b[:, lanes(i)]) - centre) * half
        act = (v + v * jnp.tanh(v)).astype(BF16)
        outer_reg_ref[:, lanes(i)] = jnp.dot(reg_out_ref[...], act, preferred_element_type=F32)


def denoise_kernel(
    own_ref, pair_ref, next_ref, initial_ref, skip_ref, reg_ref, pair_skip_ref, pair_reg_ref,
    outer_skip_ref, outer_reg_ref, diff_in_ref, diff_skip_ref, diff_mid_ref, diff_out_ref, embed_ref,
    mean_ref, band_ref, send_pair_ref, send_next_ref,
    taps_in, skips, base, hidden, taps,
):
    even, first, last = place()
    sample = lax.axis_index("segment")
    clear_edges(taps)

    def rows_of(ref):
        block = ref[sample].astype(F32)
        return [block[:, r, :] for r in range(block.shape[1])]

    own = [own_ref[:, lanes(r)] for r in range(BAND)]
    pair, across = (rows_of(ref) for ref in (pair_ref, next_ref))
    coarse = [jnp.where(even, across[2 + i], pair[2 + i]) for i in range(2)]
    coarse += own
    coarse += [jnp.where(even, pair[i], across[i]) for i in range(2)]
    reg = [reg_ref[:, lanes(r)] for r in range(ROWS)]
    up = [jnp.where(even, outer_reg_ref[:, lanes(i)], pair_reg_ref[:, lanes(i)]) for i in range(4)]
    down = [jnp.where(even, pair_reg_ref[:, lanes(i)], outer_reg_ref[:, lanes(i)]) for i in range(4)]
    mean = []
    for r in range(ROWS):
        both = 0.5 * (reg[r] + (up[r] if r < 4 else down[r - 4]))
        if r < MARGIN:
            mean.append(jnp.where(first, jnp.zeros_like(both), both))
        elif r < 4:
            mean.append(jnp.where(first, reg[r], both))
        elif r < MARGIN + BAND:
            mean.append(jnp.where(last, reg[r], both))
        else:
            mean.append(jnp.where(last, jnp.zeros_like(both), both))
    for i in range(BAND):
        mean_ref[:, lanes(i)] = mean[MARGIN + i]
    mean = [m.astype(BF16).astype(F32) for m in mean]
    for i in range(2):
        coarse[i] = jnp.where(first, jnp.zeros_like(coarse[i]), coarse[i])
        coarse[6 + i] = jnp.where(last, jnp.zeros_like(coarse[i]), coarse[6 + i])
        low = jnp.where(even, outer_skip_ref[:, lanes(i)], pair_skip_ref[:, lanes(i)])
        high = jnp.where(even, pair_skip_ref[:, lanes(i)], outer_skip_ref[:, lanes(i)])
        skips[:, lanes(i)] = jnp.where(first, jnp.zeros_like(low), low)
        skips[:, lanes(6 + i)] = jnp.where(last, jnp.zeros_like(high), high)
    skips[:, lanes(MARGIN, BAND)] = skip_ref[...]
    base[...] = jnp.dot(diff_skip_ref[...], skips[...], preferred_element_type=F32)

    channels = diff_mid_ref.shape[0]
    embed = jnp.broadcast_to(embed_ref[...], (LANES, channels)).T
    initial = [initial_ref[:, lanes(r)] for r in range(ROWS)]
    step = 2

    def denoise(current, sigma_now):
        total_var = sigma_now * sigma_now + sigma_data * sigma_data
        input_scale = 1.0 / math.sqrt(total_var)
        skip_coef = sigma_data * sigma_data / total_var
        out_coef = sigma_now * sigma_data / math.sqrt(total_var)
        input_taps(
            [
                jnp.concatenate([input_scale * current[r], coarse[r], mean[r]], axis=0)
                for r in range(ROWS)
            ],
            taps_in,
        )
        shift = (math.log(sigma_now) / 4.0) * embed
        for r in range(0, ROWS, step):
            hidden[:, lanes(r, step)] = (
                jnp.dot(diff_in_ref[...], taps_in[:, lanes(r, step)], preferred_element_type=F32)
                + base[:, lanes(r, step)]
                + jnp.concatenate([shift] * step, axis=1)
            )
        scales = norm_scales(hidden)
        for r in range(ROWS):
            store_row(taps, r, act_row(hidden, r, scales))
        for r in range(0, ROWS, step):
            hidden[:, lanes(r, step)] += conv_rows(
                lambda at, depth: diff_mid_ref[:, at : at + depth], taps, r, step
            )
        scales = norm_scales(hidden)
        result = []
        for r in range(ROWS):
            act = act_row(hidden, r, scales).astype(BF16)
            out = jnp.dot(diff_out_ref[...], act, preferred_element_type=F32)
            result.append(skip_coef * current[r] + out_coef * out)
        return result

    denoised = denoise(initial, sigma_high)
    stepped = [
        x + (sigma_low - sigma_high) * (x - d) / sigma_high for x, d in zip(initial, denoised)
    ]
    final = denoise(stepped, sigma_low)
    for i in range(BAND):
        band_ref[:, lanes(i)] = final[MARGIN + i]
    for i in range(MARGIN):
        send_pair_ref[:, lanes(i)] = jnp.where(even, final[6 + i], final[i])
        send_next_ref[:, lanes(i)] = jnp.where(even, final[i], final[6 + i])


def average_kernel(mean_ref, band_ref, pair_ref, next_ref, own_ref, send_ref):
    even, first, last = place()
    lower = lax.axis_index("segment") == 0
    for i in range(BAND):
        here = band_ref[:, lanes(i)]
        mean = mean_ref[:, lanes(i)]
        j = i % MARGIN
        if i < MARGIN:
            other = jnp.where(even, next_ref[:, lanes(j)], pair_ref[:, lanes(j)])
            alone = first
        else:
            other = jnp.where(even, pair_ref[:, lanes(j)], next_ref[:, lanes(j)])
            alone = last
        value = jnp.where(alone, here, 0.5 * (here + other)) + mean.astype(BF16).astype(F32)
        own_ref[:, i, :] = jnp.where(lower, mean, value)
        send_ref[:, i, :] = jnp.where(lower, value, mean)


def output_kernel(own_ref, got_ref, out_ref):
    lower = lax.axis_index("segment") == 0
    own, got = own_ref[...], got_ref[...]
    out_ref[0, 0] = jnp.where(lower, own, got)
    out_ref[0, 1] = jnp.where(lower, got, own)


def call(kernel, name, outs, scratch=(), flops=0):
    return pl.pallas_call(
        kernel,
        name=name,
        out_shape=[jax.ShapeDtypeStruct(shape, dtype) for shape, dtype in outs],
        scratch_shapes=scratch,
        compiler_params=pltpu.CompilerParams(vmem_limit_bytes=24 * 1024 * 1024),
        cost_estimate=pl.CostEstimate(flops=flops, bytes_accessed=0, transcendentals=0),
    )


def shards(
    coarse, noise_draw, reg_in, reg_mid, reg_out, diff_in, diff_skip, diff_mid, diff_out, noise_embed
):
    tiles, segments = lax.axis_size("tile"), lax.axis_size("segment")
    grid = [(s, t) for s in range(segments) for t in range(tiles)]

    def permute(value, target):
        edges = [(s * tiles + t, target(s, t)[0] * tiles + target(s, t)[1]) for s, t in grid]
        return lax.ppermute(value, ("segment", "tile"), edges)

    def pair(s, t):
        return s, t ^ 1

    def across(s, t):
        to = t - 1 if t % 2 == 0 else t + 1
        return (s, to) if 0 <= to < tiles else ((s + 1) % segments, t)

    def far(s, t):
        to = t + 2 if t % 2 == 0 else t - 2
        return s, min(max(to, 0), tiles - 1)

    def other(s, t):
        return (s + 1) % segments, t

    width_r, width_d, fields, inputs = reg_in.shape[0], diff_in.shape[0], reg_out.shape[0], coarse.shape[1]
    cells, band_cells, edge_cells = ROWS * LANES, BAND * LANES, MARGIN * LANES
    taps_cells = cells + 2 * LANES

    pair_coarse = permute(coarse, pair)
    next_coarse = permute(coarse, across)
    far_coarse = permute(coarse, far)
    own_coarse, initial = call(
        prepare_kernel, "prepare", [((inputs, band_cells), F32), ((fields, cells), F32)], flops=4 * 10**9
    )(coarse, noise_draw)
    skip, reg, send_skip, send_reg, outer_skip, outer_reg = call(
        regress_kernel,
        "regress",
        [
            ((width_r, band_cells), BF16),
            ((fields, cells), F32),
            ((width_r, edge_cells), BF16),
            ((fields, band_cells), F32),
            ((width_r, edge_cells), BF16),
            ((fields, band_cells), F32),
        ],
        [
            pltpu.VMEM((reg_in.shape[1], cells), BF16),
            pltpu.VMEM((width_r, cells), F32),
            pltpu.VMEM((width_r, cells), F32),
            pltpu.VMEM((3 * width_r, taps_cells), BF16),
            pltpu.VMEM((3 * width_r, taps_cells), BF16),
        ],
        flops=4 * 10**9,
    )(own_coarse, pair_coarse, next_coarse, far_coarse, reg_in, reg_mid, reg_out)
    pair_skip = permute(send_skip, pair)
    pair_reg = permute(send_reg, pair)
    mean, band, send_pair, send_next = call(
        denoise_kernel,
        "denoise",
        [
            ((fields, band_cells), F32),
            ((fields, band_cells), F32),
            ((fields, edge_cells), F32),
            ((fields, edge_cells), F32),
        ],
        [
            pltpu.VMEM((diff_in.shape[1], cells), BF16),
            pltpu.VMEM((width_r, cells), BF16),
            pltpu.VMEM((width_d, cells), F32),
            pltpu.VMEM((width_d, cells), F32),
            pltpu.VMEM((3 * width_d, taps_cells), BF16),
        ],
        flops=4 * 10**9,
    )(
        own_coarse, pair_coarse, next_coarse, initial, skip, reg, pair_skip, pair_reg,
        outer_skip, outer_reg, diff_in, diff_skip, diff_mid, diff_out, noise_embed[None],
    )
    pair_band = permute(send_pair, pair)
    next_band = permute(send_next, across)
    piece = ((fields, BAND, LANES), F32)
    own, send = call(average_kernel, "average", [piece, piece])(mean, band, pair_band, next_band)
    got = permute(send, other)
    (out,) = call(output_kernel, "output", [((1, 2, fields, BAND, LANES), F32)])(own, got)
    return out


def solution(mesh):
    return jax.shard_map(
        shards,
        mesh=mesh,
        in_specs=(P(None, None, "tile", None), P(None, None, "tile", None)) + (P(),) * 8,
        out_specs=P("segment", None, None, "tile", None),
        check_vma=False,
    )
```

```python
import math

import jax
import jax.numpy as jnp
from jax import lax
from jax.experimental import pallas as pl
from jax.experimental.pallas import tpu as pltpu
from jax.sharding import PartitionSpec as P

GROUPS = 32
LANES = 128
BAND = 4
MARGIN = 2
ROWS = BAND + 2 * MARGIN
STEP = 2
TILE = 256

sigma_high = 4.0
sigma_low = 0.5
sigma_data = 0.5

F32 = jnp.float32
BF16 = jnp.bfloat16


def lanes(first, count=1):
    return slice(first * LANES, (first + count) * LANES)


def col_shifts(chunk):
    index = jnp.int16 if chunk.dtype == BF16 else jnp.int32
    lane = lax.broadcasted_iota(index, chunk.shape, 1)
    zero = jnp.zeros_like(chunk)
    before = jnp.where(lane == 0, zero, pltpu.roll(chunk, 1, 1))
    after = jnp.where(lane == LANES - 1, zero, pltpu.roll(chunk, LANES - 1, 1))
    return before, chunk, after


def group_total(part):
    channels = part.shape[0]
    size = channels // GROUPS
    if size == 8:
        total = jnp.sum(part.reshape(GROUPS, 8, LANES), axis=(1, 2), keepdims=True)
        return jnp.broadcast_to(total, (GROUPS, 8, LANES)).reshape(channels, LANES)
    blocks = channels // 24
    tiles = part.reshape(blocks, 3, 8, LANES)
    row = lax.broadcasted_iota(jnp.int32, (blocks, 8, LANES), 1)
    v0, v1, v2 = tiles[:, 0], tiles[:, 1], tiles[:, 2]
    zero = jnp.zeros_like(v0)
    sums = (
        jnp.where(row < 6, v0, zero),
        jnp.where(row >= 6, v0, zero) + jnp.where(row < 4, v1, zero),
        jnp.where(row >= 4, v1, zero) + jnp.where(row < 2, v2, zero),
        jnp.where(row >= 2, v2, zero),
    )
    t0, t1, t2, t3 = (
        jnp.broadcast_to(jnp.sum(s, axis=(1, 2), keepdims=True), (blocks, 8, LANES)) for s in sums
    )
    m0 = jnp.where(row < 6, t0, t1)
    m1 = jnp.where(row < 4, t1, t2)
    m2 = jnp.where(row < 2, t2, t3)
    return jnp.stack([m0, m1, m2], axis=1).reshape(channels, LANES)


class Norm:
    def __init__(self, channels):
        self.size = channels // GROUPS * LANES
        self.shift = None

    def add(self, chunk):
        rows = [chunk[:, lanes(r)] for r in range(STEP)]
        if self.shift is None:
            self.shift = group_total(sum(rows[1:], rows[0])) * (1.0 / (STEP * self.size))
            self.first = self.second = jnp.zeros_like(self.shift)
        for row in rows:
            away = row - self.shift
            self.first = self.first + away
            self.second = self.second + away * away

    def scales(self):
        share = 1.0 / (ROWS * self.size)
        mean = group_total(self.first) * share
        square = group_total(self.second) * share
        return self.shift + mean, 0.5 * lax.rsqrt(square - mean * mean + 1e-5)


def silu(rows, scales):
    centre, half = scales
    v = (rows - centre) * half
    return (v + v * jnp.tanh(v)).astype(BF16)


def depths(channels):
    whole = 3 * channels // TILE * TILE
    return whole, 3 * channels - whole


def packed(weight):
    whole, rest = depths(weight.shape[0])
    starts = [a * (whole + rest) for a in range(3)]
    parts = [weight[:, at : at + whole] for at in starts]
    if rest:
        parts += [weight[:, at + whole : at + whole + rest] for at in starts]
    return jnp.concatenate(parts, axis=1)


def patch_shapes(channels):
    whole, rest = depths(channels)
    hidden = [((channels, STEP * LANES), F32)] * (ROWS // STEP)
    taps = [((whole, LANES), BF16)] * ROWS
    return hidden, taps, [((3 * rest, LANES), BF16)] * ROWS if rest else []


class Patch:
    def __init__(self, hidden, hidden_next, taps, left):
        self.hidden, self.hidden_next, self.taps, self.left = hidden, hidden_next, taps, left
        self.channels = hidden[0].shape[0]
        self.whole, self.rest = depths(self.channels)

    def start(self, first_rows):
        norm = Norm(self.channels)
        for k, ref in enumerate(self.hidden):
            chunk = first_rows(k * STEP)
            ref[...] = chunk
            norm.add(chunk)
        self.scales = norm.scales()
        if self.rest:
            blank = jnp.zeros((self.rest, LANES), BF16)
            self.left[0][: self.rest, :] = blank
            self.left[-1][2 * self.rest :, :] = blank

    def rows(self, row):
        return self.hidden[row // STEP][:, lanes(row % STEP)]

    def store(self, row):
        shifts = jnp.concatenate(col_shifts(silu(self.rows(row), self.scales)), axis=0)
        self.taps[row][...] = shifts[: self.whole]
        if self.rest:
            for a in range(3):
                if 0 <= row + 1 - a < ROWS:
                    self.left[row + 1 - a][a * self.rest : (a + 1) * self.rest, :] = shifts[self.whole :]

    def act_steps(self):
        return [lambda r=r: self.store(r) for r in range(ROWS)]

    def conv_steps(self, weight):
        norm = Norm(self.channels)
        source, target = self.hidden, self.hidden_next

        def tap_row(r):
            return self.taps[r][...] if 0 <= r < ROWS else jnp.zeros((self.whole, LANES), BF16)

        def step(k):
            first = k * STEP
            taps = [
                jnp.concatenate([tap_row(first + i + a - 1) for i in range(STEP)], axis=1) for a in range(3)
            ]
            if self.rest:
                taps.append(jnp.concatenate([self.left[first + i][...] for i in range(STEP)], axis=1))
            chunk = source[k][...] + jnp.dot(
                weight(), jnp.concatenate(taps, axis=0), preferred_element_type=F32
            )
            target[k][...] = chunk
            norm.add(chunk)
            if k == len(source) - 1:
                self.scales = norm.scales()
                self.hidden, self.hidden_next = target, source

        return [lambda k=k: step(k) for k in range(len(source))]


def run(*columns):
    longest = max(len(c) for c in columns)
    done = [0] * len(columns)
    for i in range(1, longest + 1):
        for k, column in enumerate(columns):
            while done[k] * longest < i * len(column):
                column[done[k]]()
                done[k] += 1


def input_taps(rows, out_ref):
    if rows[0].shape[0] % 16 == 0:
        rows = [row.astype(BF16) for row in rows]
    shifted = [col_shifts(row) for row in rows]
    blank = jnp.zeros_like(rows[0])
    for i in range(ROWS):
        pieces = []
        for a in range(3):
            pieces.extend(shifted[i + a - 1] if 0 <= i + a - 1 < ROWS else [blank] * 3)
        out_ref[:, lanes(i)] = jnp.concatenate(pieces, axis=0).astype(BF16)


def place():
    tile = lax.axis_index("tile")
    count = lax.axis_size("tile")
    return lax.rem(tile, 2) == 0, tile == 0, tile == count - 1


def prepare_kernel(embed_ref, embed_out):
    embed_out[...] = jnp.broadcast_to(embed_ref[...], embed_out.shape[::-1]).T


def weights_kernel(
    embed_ref, reg_in_ref, reg_mid_ref, diff_in_ref, diff_skip_ref,
    reg_in_out, reg_mid_out, diff_in_out, diff_skip_out,
):
    for source, target in (
        (reg_in_ref, reg_in_out), (diff_in_ref, diff_in_out), (diff_skip_ref, diff_skip_out)
    ):
        target[...] = source[...].astype(F32).T.astype(BF16)
    for block in range(reg_mid_ref.shape[0]):
        reg_mid_out[block] = packed(reg_mid_ref[block])


def coarse_window(coarse_ref, pair_ref, next_ref, far_ref):
    even, first, last = place()
    sample = lax.axis_index("segment")
    own, pair, across, far = (
        [ref[sample].astype(F32)[:, r, :] for r in range(BAND)]
        for ref in (coarse_ref, pair_ref, next_ref, far_ref)
    )
    alone = jnp.logical_or(jnp.logical_and(even, first), jnp.logical_and(jnp.logical_not(even), last))
    across, far = ([jnp.where(alone, jnp.zeros_like(r), r) for r in rows] for rows in (across, far))
    low = far[2:] + across + own + pair[:2]
    high = pair[2:] + own + across + far[:2]
    return even, [jnp.where(even, a, b) for a, b in zip(low, high)]


def own_rows(even, window):
    return [jnp.where(even, window[i + BAND], window[i]) for i in range(ROWS)]


def regress_kernel(
    coarse_ref, pair_ref, next_ref, far_ref, reg_in_ref, reg_mid_ref, reg_out_ref,
    rows_ref, skip_ref, reg_ref, send_skip_ref, send_reg_ref, *refs,
):
    taps_in_a, taps_in_b = refs[-2:]
    even, window = coarse_window(coarse_ref, pair_ref, next_ref, far_ref)
    rows_a = own_rows(even, window)
    rows_b = [jnp.where(even, window[i], window[i + BAND]) for i in range(ROWS)]
    for r in range(ROWS):
        rows_ref[:, lanes(r)] = rows_a[r]
    half = ROWS // STEP
    hidden_out, taps_out, left_out = refs[:half], refs[half : half + ROWS], refs[half + ROWS : half + 2 * ROWS]
    refs = refs[half + 2 * ROWS : -2]
    spare, refs = refs[:half], refs[half:]
    blocks = reg_mid_ref.shape[0]
    hidden_b = (spare, hidden_out) if blocks % 2 == 0 else (hidden_out, spare)
    outer = Patch(*hidden_b, taps_out, left_out)
    own = Patch(refs[:half], refs[half : 2 * half], refs[2 * half : 2 * half + ROWS], refs[2 * half + ROWS :])
    reg_in = reg_in_ref[...]
    for patch, rows, taps_in in ((own, rows_a, taps_in_a), (outer, rows_b, taps_in_b)):
        input_taps(rows, taps_in)
        patch.start(
            lambda r: jnp.dot(reg_in, taps_in[:, lanes(r, STEP)], preferred_element_type=F32)
        )

    for block in range(blocks):
        def weight():
            return reg_mid_ref[block]

        if block == 0:
            run(own.act_steps())
        run(own.conv_steps(weight), outer.act_steps())
        if block < blocks - 1:
            run(outer.conv_steps(weight), own.act_steps())

    for i in range(BAND):
        skip_ref[:, lanes(i)] = own.rows(MARGIN + i).astype(BF16)
    for i in range(MARGIN):
        send_skip_ref[:, lanes(i)] = jnp.where(even, own.rows(4 + i), own.rows(2 + i)).astype(BF16)
    reg = []
    for hidden in own.hidden:
        act = silu(hidden[...], [jnp.concatenate([s] * STEP, axis=1) for s in own.scales])
        reg.append(jnp.dot(reg_out_ref[...], act, preferred_element_type=F32))
    for k, part in enumerate(reg):
        reg_ref[:, lanes(k * STEP, STEP)] = part
    for k in range(half // 2):
        send_reg_ref[:, lanes(k * STEP, STEP)] = jnp.where(even, reg[half // 2 + k], reg[k])


def outer_kernel(reg_mid_ref, reg_out_ref, *refs):
    even, first, last = place()
    half = ROWS // STEP
    outer_skip_ref, outer_reg_ref = refs[half + 2 * ROWS : half + 2 * ROWS + 2]
    outer = Patch(
        refs[:half], refs[half + 2 * ROWS + 2 :], refs[half : half + ROWS], refs[half + ROWS : half + 2 * ROWS]
    )
    block = reg_mid_ref.shape[0] - 1
    run(outer.conv_steps(lambda: reg_mid_ref[block]))
    for i in range(MARGIN):
        outer_skip_ref[:, lanes(i)] = jnp.where(even, outer.rows(4 + i), outer.rows(2 + i)).astype(BF16)
    scales = [jnp.concatenate([s] * STEP, axis=1) for s in outer.scales]
    for k in range(half // 2):
        rows = jnp.where(even, outer.hidden[half // 2 + k][...], outer.hidden[k][...])
        outer_reg_ref[:, lanes(k * STEP, STEP)] = jnp.dot(
            reg_out_ref[...], silu(rows, scales), preferred_element_type=F32
        )


def denoise_kernel(
    rows_ref, noise_ref, skip_ref, reg_ref, pair_skip_ref, pair_reg_ref,
    outer_skip_ref, outer_reg_ref, diff_in_ref, diff_skip_ref, diff_mid_ref, diff_out_ref, embed_ref,
    mean_ref, band_ref, send_pair_ref, send_next_ref,
    taps_in, skips, base, *refs,
):
    even, first, last = place()
    coarse = [rows_ref[:, lanes(r)] for r in range(ROWS)]
    reg = [reg_ref[:, lanes(r)] for r in range(ROWS)]
    up = [jnp.where(even, outer_reg_ref[:, lanes(i)], pair_reg_ref[:, lanes(i)]) for i in range(4)]
    down = [jnp.where(even, pair_reg_ref[:, lanes(i)], outer_reg_ref[:, lanes(i)]) for i in range(4)]
    mean = []
    for r in range(ROWS):
        both = 0.5 * (reg[r] + (up[r] if r < 4 else down[r - 4]))
        if r < MARGIN:
            mean.append(jnp.where(first, jnp.zeros_like(both), both))
        elif r < 4:
            mean.append(jnp.where(first, reg[r], both))
        elif r < MARGIN + BAND:
            mean.append(jnp.where(last, reg[r], both))
        else:
            mean.append(jnp.where(last, jnp.zeros_like(both), both))
    for i in range(BAND):
        mean_ref[:, lanes(i)] = mean[MARGIN + i]
    mean = [m.astype(BF16).astype(F32) for m in mean]
    for i in range(2):
        low = jnp.where(even, outer_skip_ref[:, lanes(i)], pair_skip_ref[:, lanes(i)])
        high = jnp.where(even, pair_skip_ref[:, lanes(i)], outer_skip_ref[:, lanes(i)])
        skips[:, lanes(i)] = jnp.where(first, jnp.zeros_like(low), low)
        skips[:, lanes(6 + i)] = jnp.where(last, jnp.zeros_like(high), high)
    skips[:, lanes(MARGIN, BAND)] = skip_ref[...]
    embed = embed_ref[...]
    noise = noise_ref[lax.axis_index("segment")]
    initial = [sigma_high * noise[:, r, :] for r in range(ROWS)]
    half = ROWS // STEP
    patch = Patch(refs[:half], refs[half : 2 * half], refs[2 * half : 2 * half + ROWS], refs[2 * half + ROWS :])

    def denoise(current, sigma_now):
        total_var = sigma_now * sigma_now + sigma_data * sigma_data
        input_scale = 1.0 / math.sqrt(total_var)
        skip_coef = sigma_data * sigma_data / total_var
        out_coef = sigma_now * sigma_data / math.sqrt(total_var)
        input_taps(
            [
                jnp.concatenate([input_scale * current[r], coarse[r], mean[r]], axis=0)
                for r in range(ROWS)
            ],
            taps_in,
        )
        shift = jnp.concatenate([(math.log(sigma_now) / 4.0) * embed] * STEP, axis=1)

        def first_rows(r):
            if sigma_now == sigma_high:
                base[:, lanes(r, STEP)] = jnp.dot(
                    diff_skip_ref[...], skips[:, lanes(r, STEP)], preferred_element_type=F32
                )
            fresh = jnp.dot(diff_in_ref[...], taps_in[:, lanes(r, STEP)], preferred_element_type=F32)
            return fresh + base[:, lanes(r, STEP)] + shift

        patch.start(first_rows)
        acts = patch.act_steps()
        convs = patch.conv_steps(lambda: diff_mid_ref[...])
        for step in acts[: STEP + 1]:
            step()
        acts = acts[STEP + 1 :]
        for step in convs:
            step()
            for _ in range(min(STEP, len(acts))):
                acts.pop(0)()
        result = []
        scales = [jnp.concatenate([s] * STEP, axis=1) for s in patch.scales]
        for k, ref in enumerate(patch.hidden):
            out = jnp.dot(diff_out_ref[...], silu(ref[...], scales), preferred_element_type=F32)
            for i in range(STEP):
                result.append(skip_coef * current[k * STEP + i] + out_coef * out[:, lanes(i)])
        return result

    denoised = denoise(initial, sigma_high)
    stepped = [
        x + (sigma_low - sigma_high) * (x - d) / sigma_high for x, d in zip(initial, denoised)
    ]
    final = denoise(stepped, sigma_low)
    for i in range(BAND):
        band_ref[:, lanes(i)] = final[MARGIN + i]
    for i in range(MARGIN):
        send_pair_ref[:, lanes(i)] = jnp.where(even, final[6 + i], final[i])
        send_next_ref[:, lanes(i)] = jnp.where(even, final[i], final[6 + i])


def average_kernel(mean_ref, band_ref, pair_ref, next_ref, own_ref, send_ref):
    even, first, last = place()
    lower = lax.axis_index("segment") == 0
    for i in range(BAND):
        here = band_ref[:, lanes(i)]
        mean = mean_ref[:, lanes(i)]
        j = i % MARGIN
        if i < MARGIN:
            other = jnp.where(even, next_ref[:, lanes(j)], pair_ref[:, lanes(j)])
            alone = first
        else:
            other = jnp.where(even, pair_ref[:, lanes(j)], next_ref[:, lanes(j)])
            alone = last
        value = jnp.where(alone, here, 0.5 * (here + other)) + mean.astype(BF16).astype(F32)
        own_ref[:, i, :] = jnp.where(lower, mean, value)
        send_ref[:, i, :] = jnp.where(lower, value, mean)


def output_kernel(own_ref, got_ref, out_ref):
    lower = lax.axis_index("segment") == 0
    own, got = own_ref[...], got_ref[...]
    out_ref[0, 0] = jnp.where(lower, own, got)
    out_ref[0, 1] = jnp.where(lower, got, own)


def scratch(buffers):
    return [pltpu.VMEM(shape, dtype) for shape, dtype in buffers]


def call(kernel, name, outs, scratch_shapes=(), flops=0):
    return pl.pallas_call(
        kernel,
        name=name,
        out_shape=[jax.ShapeDtypeStruct(shape, dtype) for shape, dtype in outs],
        scratch_shapes=scratch_shapes,
        compiler_params=pltpu.CompilerParams(vmem_limit_bytes=24 * 1024 * 1024),
        cost_estimate=pl.CostEstimate(flops=flops, bytes_accessed=0, transcendentals=0),
    )


def shards(
    coarse, noise_draw, reg_in, reg_mid, reg_out, diff_in, diff_skip, diff_mid, diff_out, noise_embed
):
    tiles, segments = lax.axis_size("tile"), lax.axis_size("segment")
    grid = [(s, t) for s in range(segments) for t in range(tiles)]

    def permute(value, target):
        edges = [(s * tiles + t, target(s, t)[0] * tiles + target(s, t)[1]) for s, t in grid]
        return lax.ppermute(value, ("segment", "tile"), edges)

    def pair(s, t):
        return s, t ^ 1

    def across(s, t):
        to = t - 1 if t % 2 == 0 else t + 1
        return (s, to) if 0 <= to < tiles else ((s + 1) % segments, t)

    def other(s, t):
        return (s + 1) % segments, t

    width_r, width_d, fields, inputs = reg_in.shape[0], diff_in.shape[0], reg_out.shape[0], coarse.shape[1]
    cells, band_cells, edge_cells = ROWS * LANES, BAND * LANES, MARGIN * LANES
    taps_cells = cells + 2 * LANES

    pair_coarse = permute(coarse, pair)
    next_coarse = permute(coarse, across)
    far_coarse = permute(pair_coarse, across)
    (embed,) = call(prepare_kernel, "prepare", [((width_d, LANES), F32)], flops=4 * 10**9)(noise_embed[None])
    reg_in, reg_mid, diff_in, diff_skip = call(
        weights_kernel,
        "weights",
        [(w.shape, BF16) for w in (reg_in, reg_mid, diff_in, diff_skip)],
        flops=4 * 10**9,
    )(embed, reg_in.T, reg_mid, diff_in.T, diff_skip.T)
    hidden_r, taps_r, left_r = patch_shapes(width_r)
    hidden_d, taps_d, left_d = patch_shapes(width_d)
    rows, skip, reg, send_skip, send_reg, *outer = call(
        regress_kernel,
        "regress",
        [
            ((inputs, cells), F32),
            ((width_r, band_cells), BF16),
            ((fields, cells), F32),
            ((width_r, edge_cells), BF16),
            ((fields, band_cells), F32),
        ]
        + hidden_r + taps_r + left_r,
        scratch(hidden_r * 3 + taps_r + left_r + [((reg_in.shape[1], cells), BF16)] * 2),
        flops=3 * 10**9,
    )(coarse, pair_coarse, next_coarse, far_coarse, reg_in, reg_mid, reg_out)
    pair_skip = permute(send_skip, pair)
    pair_reg = permute(send_reg, pair)
    outer_skip, outer_reg = call(
        outer_kernel,
        "outer",
        [((width_r, edge_cells), BF16), ((fields, band_cells), F32)],
        scratch(hidden_r),
        flops=10**9,
    )(reg_mid, reg_out, *outer)
    mean, band, send_pair, send_next = call(
        denoise_kernel,
        "denoise",
        [
            ((fields, band_cells), F32),
            ((fields, band_cells), F32),
            ((fields, edge_cells), F32),
            ((fields, edge_cells), F32),
        ],
        scratch(
            [((diff_in.shape[1], cells), BF16), ((width_r, cells), BF16), ((width_d, cells), F32)]
            + hidden_d * 2 + taps_d + left_d
        ),
        flops=4 * 10**9,
    )(
        rows, noise_draw, skip, reg, pair_skip, pair_reg,
        outer_skip, outer_reg, diff_in, diff_skip, diff_mid, diff_out, embed,
    )
    pair_band = permute(send_pair, pair)
    next_band = permute(send_next, across)
    piece = ((fields, BAND, LANES), F32)
    own, send = call(average_kernel, "average", [piece, piece])(mean, band, pair_band, next_band)
    got = permute(send, other)
    (out,) = call(output_kernel, "output", [((1, 2, fields, BAND, LANES), F32)])(own, got)
    return out


def solution(mesh):
    return jax.shard_map(
        shards,
        mesh=mesh,
        in_specs=(P(None, None, "tile", None), P(None, None, "tile", None)) + (P(),) * 8,
        out_specs=P("segment", None, None, "tile", None),
        check_vma=False,
    )
```

```python
import math

import jax
import jax.numpy as jnp
from jax import lax
from jax.experimental import pallas as pl
from jax.experimental.pallas import tpu as pltpu
from jax.sharding import PartitionSpec as P

GROUPS = 32
LANES = 128
BAND = 4
MARGIN = 2
ROWS = BAND + 2 * MARGIN
STEP = 2
TILE = 256

sigma_high = 4.0
sigma_low = 0.5
sigma_data = 0.5

F32 = jnp.float32
BF16 = jnp.bfloat16


def lanes(first, count=1):
    return slice(first * LANES, (first + count) * LANES)


def col_shifts(chunk):
    index = jnp.int16 if chunk.dtype == BF16 else jnp.int32
    lane = lax.broadcasted_iota(index, chunk.shape, 1)
    zero = jnp.zeros_like(chunk)
    before = jnp.where(lane == 0, zero, pltpu.roll(chunk, 1, 1))
    after = jnp.where(lane == LANES - 1, zero, pltpu.roll(chunk, LANES - 1, 1))
    return before, chunk, after


def group_total(part):
    channels = part.shape[0]
    size = channels // GROUPS
    if size == 8:
        total = jnp.sum(part.reshape(GROUPS, 8, LANES), axis=(1, 2), keepdims=True)
        return jnp.broadcast_to(total, (GROUPS, 8, LANES)).reshape(channels, LANES)
    blocks = channels // 24
    tiles = part.reshape(blocks, 3, 8, LANES)
    row = lax.broadcasted_iota(jnp.int32, (blocks, 8, LANES), 1)
    v0, v1, v2 = tiles[:, 0], tiles[:, 1], tiles[:, 2]
    zero = jnp.zeros_like(v0)
    sums = (
        jnp.where(row < 6, v0, zero),
        jnp.where(row >= 6, v0, zero) + jnp.where(row < 4, v1, zero),
        jnp.where(row >= 4, v1, zero) + jnp.where(row < 2, v2, zero),
        jnp.where(row >= 2, v2, zero),
    )
    t0, t1, t2, t3 = (
        jnp.broadcast_to(jnp.sum(s, axis=(1, 2), keepdims=True), (blocks, 8, LANES)) for s in sums
    )
    m0 = jnp.where(row < 6, t0, t1)
    m1 = jnp.where(row < 4, t1, t2)
    m2 = jnp.where(row < 2, t2, t3)
    return jnp.stack([m0, m1, m2], axis=1).reshape(channels, LANES)


class Norm:
    def __init__(self, channels):
        self.size = channels // GROUPS * LANES
        self.shift = None

    def add(self, chunk):
        rows = [chunk[:, lanes(r)] for r in range(STEP)]
        if self.shift is None:
            self.shift = group_total(sum(rows[1:], rows[0])) * (1.0 / (STEP * self.size))
            self.first = self.second = jnp.zeros_like(self.shift)
        for row in rows:
            away = row - self.shift
            self.first = self.first + away
            self.second = self.second + away * away

    def scales(self):
        share = 1.0 / (ROWS * self.size)
        mean = group_total(self.first) * share
        square = group_total(self.second) * share
        return self.shift + mean, 0.5 * lax.rsqrt(square - mean * mean + 1e-5)


def silu(rows, scales):
    centre, half = scales
    v = (rows - centre) * half
    return (v + v * jnp.tanh(v)).astype(BF16)


def depths(channels):
    whole = 3 * channels // TILE * TILE
    return whole, 3 * channels - whole


def packed(weight):
    whole, rest = depths(weight.shape[0])
    starts = [a * (whole + rest) for a in range(3)]
    parts = [weight[:, at : at + whole] for at in starts]
    if rest:
        parts += [weight[:, at + whole : at + whole + rest] for at in starts]
    return jnp.concatenate(parts, axis=1)


def patch_shapes(channels):
    whole, rest = depths(channels)
    hidden = [((channels, STEP * LANES), F32)] * (ROWS // STEP)
    taps = [((whole, LANES), BF16)] * ROWS
    return hidden, taps, [((3 * rest, LANES), BF16)] * ROWS if rest else []


class Patch:
    def __init__(self, hidden, hidden_next, taps, left):
        self.hidden, self.hidden_next, self.taps, self.left = hidden, hidden_next, taps, left
        self.channels = hidden[0].shape[0]
        self.whole, self.rest = depths(self.channels)

    def start_steps(self, first_rows):
        norm = Norm(self.channels)

        def step(k):
            chunk = first_rows(k * STEP)
            self.hidden[k][...] = chunk
            norm.add(chunk)
            if k == len(self.hidden) - 1:
                self.scales = norm.scales()
                if self.rest:
                    blank = jnp.zeros((self.rest, LANES), BF16)
                    self.left[0][: self.rest, :] = blank
                    self.left[-1][2 * self.rest :, :] = blank

        return [lambda k=k: step(k) for k in range(len(self.hidden))]

    def rows(self, row):
        return self.hidden[row // STEP][:, lanes(row % STEP)]

    def store(self, row):
        shifts = jnp.concatenate(col_shifts(silu(self.rows(row), self.scales)), axis=0)
        self.taps[row][...] = shifts[: self.whole]
        if self.rest:
            for a in range(3):
                if 0 <= row + 1 - a < ROWS:
                    self.left[row + 1 - a][a * self.rest : (a + 1) * self.rest, :] = shifts[self.whole :]

    def act_steps(self):
        return [lambda r=r: self.store(r) for r in range(ROWS)]

    def conv_steps(self, weight):
        norm = Norm(self.channels)
        source, target = self.hidden, self.hidden_next

        def tap_row(r):
            return self.taps[r][...] if 0 <= r < ROWS else jnp.zeros((self.whole, LANES), BF16)

        def step(k):
            first = k * STEP
            taps = [
                jnp.concatenate([tap_row(first + i + a - 1) for i in range(STEP)], axis=1) for a in range(3)
            ]
            if self.rest:
                taps.append(jnp.concatenate([self.left[first + i][...] for i in range(STEP)], axis=1))
            chunk = source[k][...] + jnp.dot(
                weight(), jnp.concatenate(taps, axis=0), preferred_element_type=F32
            )
            target[k][...] = chunk
            norm.add(chunk)
            if k == len(source) - 1:
                self.scales = norm.scales()
                self.hidden, self.hidden_next = target, source

        return [lambda k=k: step(k) for k in range(len(source))]


def run(*columns):
    longest = max(len(c) for c in columns)
    done = [0] * len(columns)
    for i in range(1, longest + 1):
        for k, column in enumerate(columns):
            while done[k] * longest < i * len(column):
                column[done[k]]()
                done[k] += 1


def input_taps(rows, out_ref):
    if rows[0].shape[0] % 16 == 0:
        rows = [row.astype(BF16) for row in rows]
    shifted = [col_shifts(row) for row in rows]
    blank = jnp.zeros_like(rows[0])
    for i in range(ROWS):
        pieces = []
        for a in range(3):
            pieces.extend(shifted[i + a - 1] if 0 <= i + a - 1 < ROWS else [blank] * 3)
        out_ref[:, lanes(i)] = jnp.concatenate(pieces, axis=0).astype(BF16)


def place():
    tile = lax.axis_index("tile")
    count = lax.axis_size("tile")
    return lax.rem(tile, 2) == 0, tile == 0, tile == count - 1


def prepare_kernel(embed_ref, embed_out):
    embed_out[...] = jnp.broadcast_to(embed_ref[...], embed_out.shape[::-1]).T


def six_rows_kernel(coarse_ref, pair_ref, mine_ref):
    even, first, last = place()
    sample = lax.axis_index("segment")
    own, pair = ([ref[sample].astype(F32)[:, r, :] for r in range(BAND)] for ref in (coarse_ref, pair_ref))
    for i, (low, high) in enumerate(zip(own + pair[:MARGIN], pair[MARGIN:] + own)):
        mine_ref[:, lanes(i)] = jnp.where(even, low, high).astype(BF16)


def weights_kernel(
    embed_ref, reg_in_ref, reg_mid_ref, diff_in_ref, diff_skip_ref,
    reg_in_out, reg_mid_out, diff_in_out, diff_skip_out,
):
    for source, target in (
        (reg_in_ref, reg_in_out), (diff_in_ref, diff_in_out), (diff_skip_ref, diff_skip_out)
    ):
        target[...] = source[...].astype(F32).T.astype(BF16)
    for block in range(reg_mid_ref.shape[0]):
        reg_mid_out[block] = packed(reg_mid_ref[block])


def coarse_window(mine_ref, across_ref):
    even, first, last = place()
    alone = jnp.logical_or(jnp.logical_and(even, first), jnp.logical_and(jnp.logical_not(even), last))
    mine, across = (
        [ref[:, lanes(i)].astype(F32) for i in range(BAND + MARGIN)] for ref in (mine_ref, across_ref)
    )
    across = [jnp.where(alone, jnp.zeros_like(r), r) for r in across]
    return even, [jnp.where(even, a, b) for a, b in zip(across + mine, mine + across)]


def own_rows(even, window):
    return [jnp.where(even, window[i + BAND], window[i]) for i in range(ROWS)]


def regress_kernel(
    mine_ref, across_ref, reg_in_ref, reg_mid_ref, reg_out_ref,
    rows_ref, skip_ref, reg_ref, send_ref, *refs,
):
    taps_in_a, taps_in_b = refs[-2:]
    even, window = coarse_window(mine_ref, across_ref)
    rows_a = own_rows(even, window)
    rows_b = [jnp.where(even, window[i], window[i + BAND]) for i in range(ROWS)]
    for r in range(ROWS):
        rows_ref[:, lanes(r)] = rows_a[r]
    half = ROWS // STEP
    hidden_out, taps_out, left_out = refs[:half], refs[half : half + ROWS], refs[half + ROWS : half + 2 * ROWS]
    refs = refs[half + 2 * ROWS : -2]
    spare, refs = refs[:half], refs[half:]
    blocks = reg_mid_ref.shape[0]
    hidden_b = (spare, hidden_out) if blocks % 2 == 0 else (hidden_out, spare)
    outer = Patch(*hidden_b, taps_out, left_out)
    own = Patch(refs[:half], refs[half : 2 * half], refs[2 * half : 2 * half + ROWS], refs[2 * half + ROWS :])
    reg_in = reg_in_ref[...]

    def in_steps(patch, rows, taps_in):
        steps = patch.start_steps(
            lambda r: jnp.dot(reg_in, taps_in[:, lanes(r, STEP)], preferred_element_type=F32)
        )
        return [lambda: input_taps(rows, taps_in)] + steps + patch.act_steps()

    run(in_steps(own, rows_a, taps_in_a))
    outer_steps = in_steps(outer, rows_b, taps_in_b)
    for block in range(blocks):
        def weight():
            return reg_mid_ref[block]

        run(own.conv_steps(weight), outer_steps)
        if block < blocks - 1:
            run(outer.conv_steps(weight), own.act_steps())
            outer_steps = outer.act_steps()

    for i in range(BAND):
        skip_ref[:, lanes(i)] = own.rows(MARGIN + i).astype(BF16)
    width = skip_ref.shape[0]
    for i in range(MARGIN):
        send_ref[:width, lanes(i)] = jnp.where(even, own.rows(4 + i), own.rows(2 + i)).astype(BF16)
    reg = []
    for hidden in own.hidden:
        act = silu(hidden[...], [jnp.concatenate([s] * STEP, axis=1) for s in own.scales])
        reg.append(jnp.dot(reg_out_ref[...], act, preferred_element_type=F32))
    for k, part in enumerate(reg):
        reg_ref[:, lanes(k * STEP, STEP)] = part
    parts = [jnp.where(even, reg[half // 2 + k], reg[k]) for k in range(half // 2)]
    tops = [part.astype(BF16).astype(F32) for part in parts]
    parts = tops + [part - top for part, top in zip(parts, tops)]
    send_ref[width:, :] = jnp.concatenate(parts, axis=0).astype(BF16)


def outer_kernel(reg_mid_ref, reg_out_ref, *refs):
    even, first, last = place()
    half = ROWS // STEP
    outer_skip_ref, outer_reg_ref = refs[half + 2 * ROWS : half + 2 * ROWS + 2]
    outer = Patch(
        refs[:half], refs[half + 2 * ROWS + 2 :], refs[half : half + ROWS], refs[half + ROWS : half + 2 * ROWS]
    )
    block = reg_mid_ref.shape[0] - 1
    run(outer.conv_steps(lambda: reg_mid_ref[block]))
    for i in range(MARGIN):
        outer_skip_ref[:, lanes(i)] = jnp.where(even, outer.rows(4 + i), outer.rows(2 + i)).astype(BF16)
    scales = [jnp.concatenate([s] * STEP, axis=1) for s in outer.scales]
    for k in range(half // 2):
        rows = jnp.where(even, outer.hidden[half // 2 + k][...], outer.hidden[k][...])
        outer_reg_ref[:, lanes(k * STEP, STEP)] = jnp.dot(
            reg_out_ref[...], silu(rows, scales), preferred_element_type=F32
        )


def denoise_kernel(
    rows_ref, noise_ref, skip_ref, reg_ref, pair_ref,
    outer_skip_ref, outer_reg_ref, diff_in_ref, diff_skip_ref, diff_mid_ref, diff_out_ref, embed_ref,
    mean_ref, band_ref, send_pair_ref, send_next_ref,
    taps_in, skips, base, *refs,
):
    even, first, last = place()
    coarse = [rows_ref[:, lanes(r)] for r in range(ROWS)]
    reg = [reg_ref[:, lanes(r)] for r in range(ROWS)]
    width, fields = skip_ref.shape[0], reg_ref.shape[0]
    parts = pair_ref[width:, :].astype(F32)
    parts = parts[: 2 * fields] + parts[2 * fields :]
    pair_reg = [parts[fields * (i // STEP) : fields * (i // STEP + 1), lanes(i % STEP)] for i in range(BAND)]
    up = [jnp.where(even, outer_reg_ref[:, lanes(i)], pair_reg[i]) for i in range(4)]
    down = [jnp.where(even, pair_reg[i], outer_reg_ref[:, lanes(i)]) for i in range(4)]
    mean = []
    for r in range(ROWS):
        both = 0.5 * (reg[r] + (up[r] if r < 4 else down[r - 4]))
        if r < MARGIN:
            mean.append(jnp.where(first, jnp.zeros_like(both), both))
        elif r < 4:
            mean.append(jnp.where(first, reg[r], both))
        elif r < MARGIN + BAND:
            mean.append(jnp.where(last, reg[r], both))
        else:
            mean.append(jnp.where(last, jnp.zeros_like(both), both))
    for i in range(BAND):
        mean_ref[:, lanes(i)] = mean[MARGIN + i]
    mean = [m.astype(BF16).astype(F32) for m in mean]
    for i in range(2):
        low = jnp.where(even, outer_skip_ref[:, lanes(i)], pair_ref[:width, lanes(i)])
        high = jnp.where(even, pair_ref[:width, lanes(i)], outer_skip_ref[:, lanes(i)])
        skips[:, lanes(i)] = jnp.where(first, jnp.zeros_like(low), low)
        skips[:, lanes(6 + i)] = jnp.where(last, jnp.zeros_like(high), high)
    skips[:, lanes(MARGIN, BAND)] = skip_ref[...]
    embed = embed_ref[...]
    noise = noise_ref[lax.axis_index("segment")]
    initial = [sigma_high * noise[:, r, :] for r in range(ROWS)]
    half = ROWS // STEP
    patch = Patch(refs[:half], refs[half : 2 * half], refs[2 * half : 2 * half + ROWS], refs[2 * half + ROWS :])

    def denoise(current, sigma_now):
        total_var = sigma_now * sigma_now + sigma_data * sigma_data
        input_scale = 1.0 / math.sqrt(total_var)
        skip_coef = sigma_data * sigma_data / total_var
        out_coef = sigma_now * sigma_data / math.sqrt(total_var)
        input_taps(
            [
                jnp.concatenate([input_scale * current[r], coarse[r], mean[r]], axis=0)
                for r in range(ROWS)
            ],
            taps_in,
        )
        shift = jnp.concatenate([(math.log(sigma_now) / 4.0) * embed] * STEP, axis=1)

        def first_rows(r):
            if sigma_now == sigma_high:
                base[:, lanes(r, STEP)] = jnp.dot(
                    diff_skip_ref[...], skips[:, lanes(r, STEP)], preferred_element_type=F32
                )
            fresh = jnp.dot(diff_in_ref[...], taps_in[:, lanes(r, STEP)], preferred_element_type=F32)
            return fresh + base[:, lanes(r, STEP)] + shift

        run(patch.start_steps(first_rows))
        acts = patch.act_steps()
        convs = patch.conv_steps(lambda: diff_mid_ref[...])
        for step in acts[: STEP + 1]:
            step()
        acts = acts[STEP + 1 :]
        for step in convs:
            step()
            for _ in range(min(STEP, len(acts))):
                acts.pop(0)()
        result = []
        scales = [jnp.concatenate([s] * STEP, axis=1) for s in patch.scales]
        for k, ref in enumerate(patch.hidden):
            out = jnp.dot(diff_out_ref[...], silu(ref[...], scales), preferred_element_type=F32)
            for i in range(STEP):
                result.append(skip_coef * current[k * STEP + i] + out_coef * out[:, lanes(i)])
        return result

    denoised = denoise(initial, sigma_high)
    stepped = [
        x + (sigma_low - sigma_high) * (x - d) / sigma_high for x, d in zip(initial, denoised)
    ]
    final = denoise(stepped, sigma_low)
    for i in range(BAND):
        band_ref[:, lanes(i)] = final[MARGIN + i]
    for i in range(MARGIN):
        send_pair_ref[:, lanes(i)] = jnp.where(even, final[6 + i], final[i])
        send_next_ref[:, lanes(i)] = jnp.where(even, final[i], final[6 + i])


def average_kernel(mean_ref, band_ref, pair_ref, next_ref, own_ref, send_ref):
    even, first, last = place()
    lower = lax.axis_index("segment") == 0
    for i in range(BAND):
        here = band_ref[:, lanes(i)]
        mean = mean_ref[:, lanes(i)]
        j = i % MARGIN
        if i < MARGIN:
            other = jnp.where(even, next_ref[:, lanes(j)], pair_ref[:, lanes(j)])
            alone = first
        else:
            other = jnp.where(even, pair_ref[:, lanes(j)], next_ref[:, lanes(j)])
            alone = last
        value = jnp.where(alone, here, 0.5 * (here + other)) + mean.astype(BF16).astype(F32)
        own_ref[:, i, :] = jnp.where(lower, mean, value)
        send_ref[:, i, :] = jnp.where(lower, value, mean)


def output_kernel(own_ref, got_ref, out_ref):
    lower = lax.axis_index("segment") == 0
    own, got = own_ref[...], got_ref[...]
    out_ref[0, 0] = jnp.where(lower, own, got)
    out_ref[0, 1] = jnp.where(lower, got, own)


def scratch(buffers):
    return [pltpu.VMEM(shape, dtype) for shape, dtype in buffers]


def call(kernel, name, outs, scratch_shapes=(), flops=0):
    return pl.pallas_call(
        kernel,
        name=name,
        out_shape=[jax.ShapeDtypeStruct(shape, dtype) for shape, dtype in outs],
        scratch_shapes=scratch_shapes,
        compiler_params=pltpu.CompilerParams(vmem_limit_bytes=24 * 1024 * 1024),
        cost_estimate=pl.CostEstimate(flops=flops, bytes_accessed=0, transcendentals=0),
    )


def shards(
    coarse, noise_draw, reg_in, reg_mid, reg_out, diff_in, diff_skip, diff_mid, diff_out, noise_embed
):
    tiles, segments = lax.axis_size("tile"), lax.axis_size("segment")
    grid = [(s, t) for s in range(segments) for t in range(tiles)]

    def permute(value, target):
        edges = [(s * tiles + t, target(s, t)[0] * tiles + target(s, t)[1]) for s, t in grid]
        return lax.ppermute(value, ("segment", "tile"), edges)

    def pair(s, t):
        return s, t ^ 1

    def across(s, t):
        to = t - 1 if t % 2 == 0 else t + 1
        return (s, to) if 0 <= to < tiles else ((s + 1) % segments, t)

    def other(s, t):
        return (s + 1) % segments, t

    width_r, width_d, fields, inputs = reg_in.shape[0], diff_in.shape[0], reg_out.shape[0], coarse.shape[1]
    cells, band_cells, edge_cells = ROWS * LANES, BAND * LANES, MARGIN * LANES
    taps_cells = cells + 2 * LANES

    pair_coarse = permute(coarse, pair)
    (embed,) = call(prepare_kernel, "prepare", [((width_d, LANES), F32)], flops=4 * 10**9)(noise_embed[None])
    (mine,) = call(six_rows_kernel, "six_rows", [((inputs, band_cells + edge_cells), BF16)])(
        coarse, pair_coarse
    )
    next_coarse = permute(mine, across)
    reg_in, reg_mid, diff_in, diff_skip = call(
        weights_kernel,
        "weights",
        [(w.shape, BF16) for w in (reg_in, reg_mid, diff_in, diff_skip)],
        flops=4 * 10**9,
    )(embed, reg_in.T, reg_mid, diff_in.T, diff_skip.T)
    hidden_r, taps_r, left_r = patch_shapes(width_r)
    hidden_d, taps_d, left_d = patch_shapes(width_d)
    rows, skip, reg, send, *outer = call(
        regress_kernel,
        "regress",
        [
            ((inputs, cells), F32),
            ((width_r, band_cells), BF16),
            ((fields, cells), F32),
            ((width_r + 2 * fields * BAND // MARGIN, edge_cells), BF16),
        ]
        + hidden_r + taps_r + left_r,
        scratch(hidden_r * 3 + taps_r + left_r + [((reg_in.shape[1], cells), BF16)] * 2),
        flops=3 * 10**9,
    )(mine, next_coarse, reg_in, reg_mid, reg_out)
    from_pair = permute(send, pair)
    outer_skip, outer_reg = call(
        outer_kernel,
        "outer",
        [((width_r, edge_cells), BF16), ((fields, band_cells), F32)],
        scratch(hidden_r),
        flops=10**9,
    )(reg_mid, reg_out, *outer)
    mean, band, send_pair, send_next = call(
        denoise_kernel,
        "denoise",
        [
            ((fields, band_cells), F32),
            ((fields, band_cells), F32),
            ((fields, edge_cells), F32),
            ((fields, edge_cells), F32),
        ],
        scratch(
            [((diff_in.shape[1], cells), BF16), ((width_r, cells), BF16), ((width_d, cells), F32)]
            + hidden_d * 2 + taps_d + left_d
        ),
        flops=4 * 10**9,
    )(
        rows, noise_draw, skip, reg, from_pair,
        outer_skip, outer_reg, diff_in, diff_skip, diff_mid, diff_out, embed,
    )
    pair_band = permute(send_pair, pair)
    next_band = permute(send_next, across)
    piece = ((fields, BAND, LANES), F32)
    own, send = call(average_kernel, "average", [piece, piece])(mean, band, pair_band, next_band)
    got = permute(send, other)
    (out,) = call(output_kernel, "output", [((1, 2, fields, BAND, LANES), F32)])(own, got)
    return out


def solution(mesh):
    return jax.shard_map(
        shards,
        mesh=mesh,
        in_specs=(P(None, None, "tile", None), P(None, None, "tile", None)) + (P(),) * 8,
        out_specs=P("segment", None, None, "tile", None),
        check_vma=False,
    )
```

```python
import math

import jax
import jax.numpy as jnp
from jax import lax
from jax.experimental import pallas as pl
from jax.experimental.pallas import tpu as pltpu
from jax.sharding import PartitionSpec as P

GROUPS = 32
LANES = 128
BAND = 4
MARGIN = 2
ROWS = BAND + 2 * MARGIN
STEP = 2
TILE = 256

sigma_high = 4.0
sigma_low = 0.5
sigma_data = 0.5

F32 = jnp.float32
BF16 = jnp.bfloat16


def lanes(first, count=1):
    return slice(first * LANES, (first + count) * LANES)


def col_shifts(chunk):
    lane = lax.broadcasted_iota(jnp.int32, chunk.shape, 1)
    zero = jnp.zeros_like(chunk)
    before = jnp.where(lane == 0, zero, pltpu.roll(chunk, 1, 1))
    after = jnp.where(lane == LANES - 1, zero, pltpu.roll(chunk, LANES - 1, 1))
    return before, chunk, after


def group_total(part, size):
    channels = part.shape[0]
    if size == 8:
        tiles = (channels // 8, 8, LANES)
        total = jnp.sum(part.reshape(tiles), axis=(1, 2), keepdims=True)
        return jnp.broadcast_to(total, tiles).reshape(channels, LANES)
    blocks = channels // 24
    tiles = part.reshape(blocks, 3, 8, LANES)
    row = lax.broadcasted_iota(jnp.int32, (blocks, 8, LANES), 1)
    v0, v1, v2 = tiles[:, 0], tiles[:, 1], tiles[:, 2]
    zero = jnp.zeros_like(v0)
    sums = (
        jnp.where(row < 6, v0, zero),
        jnp.where(row >= 6, v0, zero) + jnp.where(row < 4, v1, zero),
        jnp.where(row >= 4, v1, zero) + jnp.where(row < 2, v2, zero),
        jnp.where(row >= 2, v2, zero),
    )
    t0, t1, t2, t3 = (
        jnp.broadcast_to(jnp.sum(s, axis=(1, 2), keepdims=True), (blocks, 8, LANES)) for s in sums
    )
    m0 = jnp.where(row < 6, t0, t1)
    m1 = jnp.where(row < 4, t1, t2)
    m2 = jnp.where(row < 2, t2, t3)
    return jnp.stack([m0, m1, m2], axis=1).reshape(channels, LANES)


class Norm:
    def __init__(self, size):
        self.size = size
        self.shift = None

    def add(self, chunk):
        rows = [chunk[:, lanes(r)] for r in range(STEP)]
        if self.shift is None:
            self.shift = group_total(sum(rows[1:], rows[0]), self.size) * (1.0 / (STEP * self.size * LANES))
            self.first = self.second = jnp.zeros_like(self.shift)
        for row in rows:
            away = row - self.shift
            self.first = self.first + away
            self.second = self.second + away * away

    def scales(self):
        share = 1.0 / (ROWS * self.size * LANES)
        mean = group_total(self.first, self.size) * share
        square = group_total(self.second, self.size) * share
        return self.shift + mean, 0.5 * lax.rsqrt(square - mean * mean + 1e-5)


def silu(rows, scales):
    centre, half = scales
    v = (rows - centre) * half
    return v + v * jnp.tanh(v)


def depths(channels):
    whole = 3 * channels // TILE * TILE
    return whole, 3 * channels - whole


def packed(weight):
    whole, rest = depths(weight.shape[0])
    starts = [a * (whole + rest) for a in range(3)]
    parts = [weight[:, at : at + whole] for at in starts]
    if rest:
        parts += [weight[:, at + whole : at + whole + rest] for at in starts]
    return jnp.concatenate(parts, axis=1)


def patch_shapes(channels):
    whole, rest = depths(channels)
    hidden = [((channels, STEP * LANES), F32)] * (ROWS // STEP)
    taps = [((whole, LANES), BF16)] * ROWS
    return hidden, taps, [((3 * rest, LANES), BF16)] * ROWS if rest else []


class Patch:
    def __init__(self, hidden, hidden_next, taps, left):
        self.hidden, self.hidden_next, self.taps, self.left = hidden, hidden_next, taps, left
        self.channels = hidden[0].shape[0]
        self.whole, self.rest = depths(self.channels)

    def start_steps(self, first_rows):
        norm = Norm(self.channels // GROUPS)

        def step(k):
            chunk = first_rows(k * STEP)
            self.hidden[k][...] = chunk
            norm.add(chunk)
            if k == len(self.hidden) - 1:
                self.scales = norm.scales()
                if self.rest:
                    blank = jnp.zeros((self.rest, LANES), BF16)
                    self.left[0][: self.rest, :] = blank
                    self.left[-1][2 * self.rest :, :] = blank

        return [lambda k=k: step(k) for k in range(len(self.hidden))]

    def rows(self, row):
        return self.hidden[row // STEP][:, lanes(row % STEP)]

    def store(self, row):
        pieces = col_shifts(silu(self.rows(row), self.scales))
        shifts = jnp.concatenate([piece.astype(BF16) for piece in pieces], axis=0)
        self.taps[row][...] = shifts[: self.whole]
        if self.rest:
            for a in range(3):
                if 0 <= row + 1 - a < ROWS:
                    self.left[row + 1 - a][a * self.rest : (a + 1) * self.rest, :] = shifts[self.whole :]

    def act_steps(self):
        return [lambda r=r: self.store(r) for r in range(ROWS)]

    def conv_steps(self, weight):
        norm = Norm(self.channels // GROUPS)
        source, target = self.hidden, self.hidden_next

        def tap_row(r):
            return self.taps[r][...] if 0 <= r < ROWS else jnp.zeros((self.whole, LANES), BF16)

        def step(k):
            first = k * STEP
            taps = [
                jnp.concatenate([tap_row(first + i + a - 1) for i in range(STEP)], axis=1) for a in range(3)
            ]
            if self.rest:
                taps.append(jnp.concatenate([self.left[first + i][...] for i in range(STEP)], axis=1))
            chunk = source[k][...] + jnp.dot(
                weight(), jnp.concatenate(taps, axis=0), preferred_element_type=F32
            )
            target[k][...] = chunk
            norm.add(chunk)
            if k == len(source) - 1:
                self.scales = norm.scales()
                self.hidden, self.hidden_next = target, source

        return [lambda k=k: step(k) for k in range(len(source))]


class SplitPatch:
    taps_order = [(a, b) for a in range(3) for b in range(3)]

    def __init__(self, hidden, taps, size):
        self.hidden, self.taps, self.size = hidden, taps, size
        self.part = hidden[0][0].shape[0]
        self.scales = [None, None]

    def columns(self, p):
        return slice(p * self.part, (p + 1) * self.part)

    def start_steps(self, p, first_rows):
        norm = Norm(self.size)

        def step(k):
            chunk = first_rows(self.columns(p), k * STEP)
            self.hidden[p][k][...] = chunk
            norm.add(chunk)
            if k == ROWS // STEP - 1:
                self.scales[p] = norm.scales()

        return [lambda k=k: step(k) for k in range(ROWS // STEP)]

    def store(self, p, row):
        chunk = silu(self.hidden[p][row // STEP][:, lanes(row % STEP)], self.scales[p])
        for b, piece in enumerate(col_shifts(chunk)):
            self.taps[p][row][self.columns(b), :] = piece.astype(BF16)

    def act_steps(self, p):
        return [lambda r=r: self.store(p, r) for r in range(ROWS)]

    def product(self, weight_ref, outs, taps, k):
        first = k * STEP
        weights, pieces = [], []
        for p, a, b in taps:
            at = ((3 * a + b) * 2 + p) * self.part
            weights.append(weight_ref[outs, at : at + self.part])
            rows = [first + i + a - 1 for i in range(STEP)]
            blank = jnp.zeros((self.part, LANES), BF16)
            pieces.append(
                jnp.concatenate(
                    [self.taps[p][r][self.columns(b), :] if 0 <= r < ROWS else blank for r in rows], axis=1
                )
            )
        return jnp.dot(
            jnp.concatenate(weights, axis=1), jnp.concatenate(pieces, axis=0), preferred_element_type=F32
        )

    def first_steps(self, weight_ref):
        def step(k):
            taps = [(0, a, b) for a, b in self.taps_order[:-1]]
            added = self.product(weight_ref, slice(0, 2 * self.part), taps, k)
            for p in range(2):
                self.hidden[p][k][...] += added[self.columns(p)]

        return [lambda k=k: step(k) for k in range(ROWS // STEP)]

    def last_steps(self, weight_ref, p):
        norm = Norm(self.size)

        def step(k):
            taps = [(1, a, b) for a, b in self.taps_order] + [(0, *self.taps_order[-1])]
            chunk = self.hidden[p][k][...] + self.product(weight_ref, self.columns(p), taps, k)
            self.hidden[p][k][...] = chunk
            norm.add(chunk)
            if k == ROWS // STEP - 1:
                self.scales[p] = norm.scales()

        return [lambda k=k: step(k) for k in range(ROWS // STEP)]


def run(*columns):
    longest = max(len(c) for c in columns)
    done = [0] * len(columns)
    for i in range(1, longest + 1):
        for k, column in enumerate(columns):
            while done[k] * longest < i * len(column):
                column[done[k]]()
                done[k] += 1


def input_taps(rows, out_ref):
    shifted = [col_shifts(row) for row in rows]
    blank = jnp.zeros_like(rows[0])
    if rows[0].shape[0] % 16 == 0:
        shifted = [[piece.astype(BF16) for piece in pieces] for pieces in shifted]
        blank = blank.astype(BF16)
    for i in range(ROWS):
        pieces = []
        for a in range(3):
            pieces.extend(shifted[i + a - 1] if 0 <= i + a - 1 < ROWS else [blank] * 3)
        out_ref[:, lanes(i)] = jnp.concatenate(pieces, axis=0).astype(BF16)


def place():
    tile = lax.axis_index("tile")
    count = lax.axis_size("tile")
    return lax.rem(tile, 2) == 0, tile == 0, tile == count - 1


def prepare_kernel(embed_ref, embed_out):
    embed_out[...] = jnp.broadcast_to(embed_ref[...], embed_out.shape[::-1]).T


def six_rows_kernel(coarse_ref, pair_ref, mine_ref):
    even, first, last = place()
    sample = lax.axis_index("segment")
    own, pair = ([ref[sample].astype(F32)[:, r, :] for r in range(BAND)] for ref in (coarse_ref, pair_ref))
    for i, (low, high) in enumerate(zip(own + pair[:MARGIN], pair[MARGIN:] + own)):
        mine_ref[:, lanes(i)] = jnp.where(even, low, high).astype(BF16)


def weights_kernel(
    embed_ref, reg_in_ref, reg_mid_ref, diff_in_ref, diff_skip_ref,
    reg_in_out, reg_mid_out, diff_in_out, diff_skip_out,
):
    for source, target in (
        (reg_in_ref, reg_in_out), (diff_in_ref, diff_in_out), (diff_skip_ref, diff_skip_out)
    ):
        target[...] = source[...].astype(F32).T.astype(BF16)
    for block in range(reg_mid_ref.shape[0]):
        reg_mid_out[block] = packed(reg_mid_ref[block])


def coarse_window(mine_ref, across_ref):
    even, first, last = place()
    alone = jnp.logical_or(jnp.logical_and(even, first), jnp.logical_and(jnp.logical_not(even), last))
    mine, across = (
        [ref[:, lanes(i)].astype(F32) for i in range(BAND + MARGIN)] for ref in (mine_ref, across_ref)
    )
    across = [jnp.where(alone, jnp.zeros_like(r), r) for r in across]
    return even, [jnp.where(even, a, b) for a, b in zip(across + mine, mine + across)]


def own_rows(even, window):
    return [jnp.where(even, window[i + BAND], window[i]) for i in range(ROWS)]


def regress_kernel(
    mine_ref, across_ref, reg_in_ref, reg_mid_ref, reg_out_ref,
    rows_ref, skip_ref, reg_ref, send_ref, *refs,
):
    taps_in_a, taps_in_b = refs[-2:]
    even, window = coarse_window(mine_ref, across_ref)
    rows_a = own_rows(even, window)
    rows_b = [jnp.where(even, window[i], window[i + BAND]) for i in range(ROWS)]
    for r in range(ROWS):
        rows_ref[:, lanes(r)] = rows_a[r]
    half = ROWS // STEP
    hidden_out, taps_out, left_out = refs[:half], refs[half : half + ROWS], refs[half + ROWS : half + 2 * ROWS]
    refs = refs[half + 2 * ROWS : -2]
    spare, refs = refs[:half], refs[half:]
    blocks = reg_mid_ref.shape[0]
    hidden_b = (spare, hidden_out) if blocks % 2 == 0 else (hidden_out, spare)
    outer = Patch(*hidden_b, taps_out, left_out)
    own = Patch(refs[:half], refs[half : 2 * half], refs[2 * half : 2 * half + ROWS], refs[2 * half + ROWS :])
    reg_in = reg_in_ref[...]

    def in_steps(patch, rows, taps_in):
        steps = patch.start_steps(
            lambda r: jnp.dot(reg_in, taps_in[:, lanes(r, STEP)], preferred_element_type=F32)
        )
        return [lambda: input_taps(rows, taps_in)] + steps + patch.act_steps()

    run(in_steps(own, rows_a, taps_in_a))
    outer_steps = in_steps(outer, rows_b, taps_in_b)
    for block in range(blocks):
        def weight():
            return reg_mid_ref[block]

        run(own.conv_steps(weight), outer_steps)
        if block < blocks - 1:
            run(outer.conv_steps(weight), own.act_steps())
            outer_steps = outer.act_steps()

    for i in range(BAND):
        skip_ref[:, lanes(i)] = own.rows(MARGIN + i).astype(BF16)
    width = skip_ref.shape[0]
    for i in range(MARGIN):
        send_ref[:width, lanes(i)] = jnp.where(even, own.rows(4 + i), own.rows(2 + i)).astype(BF16)
    reg = []
    for hidden in own.hidden:
        act = silu(hidden[...], [jnp.concatenate([s] * STEP, axis=1) for s in own.scales]).astype(BF16)
        reg.append(jnp.dot(reg_out_ref[...], act, preferred_element_type=F32))
    for k, part in enumerate(reg):
        reg_ref[:, lanes(k * STEP, STEP)] = part
    parts = [jnp.where(even, reg[half // 2 + k], reg[k]) for k in range(half // 2)]
    parts = [part[:, lanes(i, MARGIN)] for part in parts for i in range(0, STEP, MARGIN)]
    tops = [part.astype(BF16).astype(F32) for part in parts]
    parts = tops + [part - top for part, top in zip(parts, tops)]
    send_ref[width:, :] = jnp.concatenate(parts, axis=0).astype(BF16)


def outer_kernel(reg_mid_ref, reg_out_ref, *refs):
    even, first, last = place()
    half = ROWS // STEP
    outer_skip_ref, outer_reg_ref = refs[half + 2 * ROWS : half + 2 * ROWS + 2]
    outer = Patch(
        refs[:half], refs[half + 2 * ROWS + 2 :], refs[half : half + ROWS], refs[half + ROWS : half + 2 * ROWS]
    )
    block = reg_mid_ref.shape[0] - 1
    run(outer.conv_steps(lambda: reg_mid_ref[block]))
    for i in range(MARGIN):
        outer_skip_ref[:, lanes(i)] = jnp.where(even, outer.rows(4 + i), outer.rows(2 + i)).astype(BF16)
    scales = [jnp.concatenate([s] * STEP, axis=1) for s in outer.scales]
    for k in range(half // 2):
        rows = jnp.where(even, outer.hidden[half // 2 + k][...], outer.hidden[k][...])
        outer_reg_ref[:, lanes(k * STEP, STEP)] = jnp.dot(
            reg_out_ref[...], silu(rows, scales).astype(BF16), preferred_element_type=F32
        )


def denoise_kernel(
    rows_ref, noise_ref, skip_ref, reg_ref, pair_ref,
    outer_skip_ref, outer_reg_ref, diff_in_ref, diff_skip_ref, diff_mid_ref, diff_out_ref, embed_ref,
    mean_ref, band_ref, send_pair_ref, send_next_ref,
    taps_in, skips, base, *refs,
):
    even, first, last = place()
    coarse = [rows_ref[:, lanes(r)] for r in range(ROWS)]
    reg = [reg_ref[:, lanes(r)] for r in range(ROWS)]
    width, fields = skip_ref.shape[0], reg_ref.shape[0]
    parts = pair_ref[width:, :].astype(F32)
    parts = parts[: 2 * fields] + parts[2 * fields :]
    pair_reg = [parts[fields * (i // MARGIN) : fields * (i // MARGIN + 1), lanes(i % MARGIN)] for i in range(BAND)]
    up = [jnp.where(even, outer_reg_ref[:, lanes(i)], pair_reg[i]) for i in range(4)]
    down = [jnp.where(even, pair_reg[i], outer_reg_ref[:, lanes(i)]) for i in range(4)]
    mean = []
    for r in range(ROWS):
        both = 0.5 * (reg[r] + (up[r] if r < 4 else down[r - 4]))
        if r < MARGIN:
            mean.append(jnp.where(first, jnp.zeros_like(both), both))
        elif r < 4:
            mean.append(jnp.where(first, reg[r], both))
        elif r < MARGIN + BAND:
            mean.append(jnp.where(last, reg[r], both))
        else:
            mean.append(jnp.where(last, jnp.zeros_like(both), both))
    for i in range(BAND):
        mean_ref[:, lanes(i)] = mean[MARGIN + i]
    mean = [m.astype(BF16).astype(F32) for m in mean]
    for i in range(2):
        low = jnp.where(even, outer_skip_ref[:, lanes(i)], pair_ref[:width, lanes(i)])
        high = jnp.where(even, pair_ref[:width, lanes(i)], outer_skip_ref[:, lanes(i)])
        skips[:, lanes(i)] = jnp.where(first, jnp.zeros_like(low), low)
        skips[:, lanes(6 + i)] = jnp.where(last, jnp.zeros_like(high), high)
    skips[:, lanes(MARGIN, BAND)] = skip_ref[...]
    embed = embed_ref[...]
    noise = noise_ref[lax.axis_index("segment")]
    initial = [sigma_high * noise[:, r, :] for r in range(ROWS)]
    half = ROWS // STEP
    patch = SplitPatch(
        (refs[:half], refs[half : 2 * half]),
        (refs[2 * half : 2 * half + ROWS], refs[2 * half + ROWS :]),
        diff_mid_ref.shape[0] // GROUPS,
    )

    def denoise(current, sigma_now):
        total_var = sigma_now * sigma_now + sigma_data * sigma_data
        input_scale = 1.0 / math.sqrt(total_var)
        skip_coef = sigma_data * sigma_data / total_var
        out_coef = sigma_now * sigma_data / math.sqrt(total_var)
        input_taps(
            [
                jnp.concatenate([input_scale * current[r], coarse[r], mean[r]], axis=0)
                for r in range(ROWS)
            ],
            taps_in,
        )
        shift = jnp.concatenate([(math.log(sigma_now) / 4.0) * embed] * STEP, axis=1)

        def first_rows(outs, r):
            if sigma_now == sigma_high:
                base[outs, lanes(r, STEP)] = jnp.dot(
                    diff_skip_ref[outs, :], skips[:, lanes(r, STEP)], preferred_element_type=F32
                )
            fresh = jnp.dot(diff_in_ref[outs, :], taps_in[:, lanes(r, STEP)], preferred_element_type=F32)
            return fresh + base[outs, lanes(r, STEP)] + shift[outs]

        run(patch.start_steps(0, first_rows))
        run(patch.start_steps(1, first_rows))
        run(patch.act_steps(0))
        run(patch.act_steps(1))
        run(patch.first_steps(diff_mid_ref))
        run(patch.last_steps(diff_mid_ref, 0))
        run(patch.last_steps(diff_mid_ref, 1))
        scales = [[jnp.concatenate([s] * STEP, axis=1) for s in part] for part in patch.scales]
        acts = []
        for k in range(half):
            pieces = [silu(patch.hidden[p][k][...], scales[p]).astype(BF16) for p in range(2)]
            acts.append(jnp.concatenate(pieces, axis=0))
        outs = jnp.dot(diff_out_ref[...], jnp.concatenate(acts, axis=1), preferred_element_type=F32)
        result = [skip_coef * current[r] + out_coef * outs[:, lanes(r)] for r in range(ROWS)]
        return result

    denoised = denoise(initial, sigma_high)
    stepped = [
        x + (sigma_low - sigma_high) * (x - d) / sigma_high for x, d in zip(initial, denoised)
    ]
    final = denoise(stepped, sigma_low)
    for i in range(BAND):
        band_ref[:, lanes(i)] = final[MARGIN + i]
    for i in range(MARGIN):
        send_pair_ref[:, lanes(i)] = jnp.where(even, final[6 + i], final[i])
        send_next_ref[:, lanes(i)] = jnp.where(even, final[i], final[6 + i])


def pair_average_kernel(band_ref, pair_ref, part_ref):
    even, first, last = place()
    for i in range(BAND):
        here = band_ref[:, lanes(i)]
        both = 0.5 * (here + pair_ref[:, lanes(i % MARGIN)])
        part_ref[:, lanes(i)] = jnp.where(even if i >= MARGIN else jnp.logical_not(even), both, here)


def average_kernel(mean_ref, part_ref, next_ref, own_ref, send_ref):
    even, first, last = place()
    lower = lax.axis_index("segment") == 0
    for i in range(BAND):
        here = part_ref[:, lanes(i)]
        mean = mean_ref[:, lanes(i)]
        both = 0.5 * (here + next_ref[:, lanes(i % MARGIN)])
        done, ends = (jnp.logical_not(even), first) if i < MARGIN else (even, last)
        value = jnp.where(jnp.logical_or(done, ends), here, both) + mean.astype(BF16).astype(F32)
        own_ref[:, i, :] = jnp.where(lower, mean, value)
        send_ref[:, i, :] = jnp.where(lower, value, mean)


def output_kernel(own_ref, got_ref, out_ref):
    lower = lax.axis_index("segment") == 0
    own, got = own_ref[...], got_ref[...]
    out_ref[0, 0] = jnp.where(lower, own, got)
    out_ref[0, 1] = jnp.where(lower, got, own)


def scratch(buffers):
    return [pltpu.VMEM(shape, dtype) for shape, dtype in buffers]


def call(kernel, name, outs, scratch_shapes=(), flops=0):
    return pl.pallas_call(
        kernel,
        name=name,
        out_shape=[jax.ShapeDtypeStruct(shape, dtype) for shape, dtype in outs],
        scratch_shapes=scratch_shapes,
        compiler_params=pltpu.CompilerParams(vmem_limit_bytes=24 * 1024 * 1024),
        cost_estimate=pl.CostEstimate(flops=flops, bytes_accessed=0, transcendentals=0),
    )


def shards(
    coarse, noise_draw, reg_in, reg_mid, reg_out, diff_in, diff_skip, diff_mid, diff_out, noise_embed
):
    tiles, segments = lax.axis_size("tile"), lax.axis_size("segment")
    grid = [(s, t) for s in range(segments) for t in range(tiles)]

    def permute(value, target):
        edges = [(s * tiles + t, target(s, t)[0] * tiles + target(s, t)[1]) for s, t in grid]
        return lax.ppermute(value, ("segment", "tile"), edges)

    def pair(s, t):
        return s, t ^ 1

    def across(s, t):
        to = t - 1 if t % 2 == 0 else t + 1
        return (s, to) if 0 <= to < tiles else ((s + 1) % segments, t)

    def other(s, t):
        return (s + 1) % segments, t

    width_r, width_d, fields, inputs = reg_in.shape[0], diff_in.shape[0], reg_out.shape[0], coarse.shape[1]
    cells, band_cells, edge_cells = ROWS * LANES, BAND * LANES, MARGIN * LANES
    taps_cells = cells + 2 * LANES

    pair_coarse = permute(coarse, pair)
    (embed,) = call(prepare_kernel, "prepare", [((width_d, LANES), F32)], flops=4 * 10**9)(noise_embed[None])
    (mine,) = call(six_rows_kernel, "six_rows", [((inputs, band_cells + edge_cells), BF16)])(
        coarse, pair_coarse
    )
    next_coarse = permute(mine, across)
    reg_in, reg_mid, diff_in, diff_skip = call(
        weights_kernel,
        "weights",
        [(w.shape, BF16) for w in (reg_in, reg_mid, diff_in, diff_skip)],
        flops=4 * 10**9,
    )(embed, reg_in.T, reg_mid, diff_in.T, diff_skip.T)
    hidden_r, taps_r, left_r = patch_shapes(width_r)
    hidden_d = [((width_d // 2, STEP * LANES), F32)] * (2 * ROWS // STEP)
    taps_d = [((3 * width_d // 2, LANES), BF16)] * (2 * ROWS)
    rows, skip, reg, send, *outer = call(
        regress_kernel,
        "regress",
        [
            ((inputs, cells), F32),
            ((width_r, band_cells), BF16),
            ((fields, cells), F32),
            ((width_r + 2 * fields * BAND // MARGIN, edge_cells), BF16),
        ]
        + hidden_r + taps_r + left_r,
        scratch(hidden_r * 3 + taps_r + left_r + [((reg_in.shape[1], cells), BF16)] * 2),
        flops=3 * 10**9,
    )(mine, next_coarse, reg_in, reg_mid, reg_out)
    from_pair = permute(send, pair)
    outer_skip, outer_reg = call(
        outer_kernel,
        "outer",
        [((width_r, edge_cells), BF16), ((fields, band_cells), F32)],
        scratch(hidden_r),
        flops=10**9,
    )(reg_mid, reg_out, *outer)
    mean, band, send_pair, send_next = call(
        denoise_kernel,
        "denoise",
        [
            ((fields, band_cells), F32),
            ((fields, band_cells), F32),
            ((fields, edge_cells), F32),
            ((fields, edge_cells), F32),
        ],
        scratch(
            [((diff_in.shape[1], cells), BF16), ((width_r, cells), BF16), ((width_d, cells), F32)]
            + hidden_d + taps_d
        ),
        flops=4 * 10**9,
    )(
        rows, noise_draw, skip, reg, from_pair,
        outer_skip, outer_reg, diff_in, diff_skip, diff_mid, diff_out, embed,
    )
    pair_band = permute(send_pair, pair)
    next_band = permute(send_next, across)
    piece = ((fields, BAND, LANES), F32)
    (part,) = call(pair_average_kernel, "pair_average", [((fields, band_cells), F32)], flops=2 * 10**9)(
        band, pair_band
    )
    own, send = call(average_kernel, "average", [piece, piece])(mean, part, next_band)
    got = permute(send, other)
    (out,) = call(output_kernel, "output", [((1, 2, fields, BAND, LANES), F32)])(own, got)
    return out


def solution(mesh):
    return jax.shard_map(
        shards,
        mesh=mesh,
        in_specs=(P(None, None, "tile", None), P(None, None, "tile", None)) + (P(),) * 8,
        out_specs=P("segment", None, None, "tile", None),
        check_vma=False,
    )
```

```python
import math

import jax
import jax.numpy as jnp
from jax import lax
from jax.experimental import pallas as pl
from jax.experimental.pallas import tpu as pltpu
from jax.sharding import PartitionSpec as P

GROUPS = 32
LANES = 128
BAND = 4
MARGIN = 2
ROWS = BAND + 2 * MARGIN
STEP = 2
TILE = 256

sigma_high = 4.0
sigma_low = 0.5
sigma_data = 0.5

F32 = jnp.float32
BF16 = jnp.bfloat16


def lanes(first, count=1):
    return slice(first * LANES, (first + count) * LANES)


def col_shifts(chunk):
    lane = lax.broadcasted_iota(jnp.int32, chunk.shape, 1)
    zero = jnp.zeros_like(chunk)
    before = jnp.where(lane == 0, zero, pltpu.roll(chunk, 1, 1))
    after = jnp.where(lane == LANES - 1, zero, pltpu.roll(chunk, LANES - 1, 1))
    return before, chunk, after


def group_total(part, size):
    channels = part.shape[0]
    if size == 8:
        tiles = (channels // 8, 8, LANES)
        total = jnp.sum(part.reshape(tiles), axis=(1, 2), keepdims=True)
        return jnp.broadcast_to(total, tiles).reshape(channels, LANES)
    blocks = channels // 24
    tiles = part.reshape(blocks, 3, 8, LANES)
    row = lax.broadcasted_iota(jnp.int32, (blocks, 8, LANES), 1)
    v0, v1, v2 = tiles[:, 0], tiles[:, 1], tiles[:, 2]
    zero = jnp.zeros_like(v0)
    sums = (
        jnp.where(row < 6, v0, zero),
        jnp.where(row >= 6, v0, zero) + jnp.where(row < 4, v1, zero),
        jnp.where(row >= 4, v1, zero) + jnp.where(row < 2, v2, zero),
        jnp.where(row >= 2, v2, zero),
    )
    t0, t1, t2, t3 = (
        jnp.broadcast_to(jnp.sum(s, axis=(1, 2), keepdims=True), (blocks, 8, LANES)) for s in sums
    )
    m0 = jnp.where(row < 6, t0, t1)
    m1 = jnp.where(row < 4, t1, t2)
    m2 = jnp.where(row < 2, t2, t3)
    return jnp.stack([m0, m1, m2], axis=1).reshape(channels, LANES)


class Norm:
    def __init__(self, size):
        self.size = size
        self.shift = None

    def add(self, chunk):
        rows = [chunk[:, lanes(r)] for r in range(STEP)]
        if self.shift is None:
            self.shift = group_total(sum(rows[1:], rows[0]), self.size) * (1.0 / (STEP * self.size * LANES))
            self.first = self.second = jnp.zeros_like(self.shift)
        for row in rows:
            away = row - self.shift
            self.first = self.first + away
            self.second = self.second + away * away

    def scales(self):
        share = 1.0 / (ROWS * self.size * LANES)
        mean = group_total(self.first, self.size) * share
        square = group_total(self.second, self.size) * share
        return self.shift + mean, 0.5 * lax.rsqrt(square - mean * mean + 1e-5)


def silu(rows, scales):
    centre, half = scales
    v = (rows - centre) * half
    return v + v * jnp.tanh(v)


def depths(channels):
    whole = 3 * channels // TILE * TILE
    return whole, 3 * channels - whole


def packed(weight):
    whole, rest = depths(weight.shape[0])
    starts = [a * (whole + rest) for a in range(3)]
    parts = [weight[:, at : at + whole] for at in starts]
    if rest:
        parts += [weight[:, at + whole : at + whole + rest] for at in starts]
    return jnp.concatenate(parts, axis=1)


def patch_shapes(channels):
    whole, rest = depths(channels)
    hidden = [((channels, STEP * LANES), F32)] * (ROWS // STEP)
    taps = [((whole, LANES), BF16)] * ROWS
    return hidden, taps, [((3 * rest, LANES), BF16)] * ROWS if rest else []


class Patch:
    def __init__(self, hidden, hidden_next, taps, left):
        self.hidden, self.hidden_next, self.taps, self.left = hidden, hidden_next, taps, left
        self.channels = hidden[0].shape[0]
        self.whole, self.rest = depths(self.channels)

    def start_steps(self, first_rows):
        norm = Norm(self.channels // GROUPS)

        def step(k):
            chunk = first_rows(k * STEP)
            self.hidden[k][...] = chunk
            norm.add(chunk)
            if k == len(self.hidden) - 1:
                self.scales = norm.scales()
                if self.rest:
                    blank = jnp.zeros((self.rest, LANES), BF16)
                    self.left[0][: self.rest, :] = blank
                    self.left[-1][2 * self.rest :, :] = blank

        return [lambda k=k: step(k) for k in range(len(self.hidden))]

    def rows(self, row):
        return self.hidden[row // STEP][:, lanes(row % STEP)]

    def store(self, row):
        pieces = col_shifts(silu(self.rows(row), self.scales))
        shifts = jnp.concatenate([piece.astype(BF16) for piece in pieces], axis=0)
        self.taps[row][...] = shifts[: self.whole]
        if self.rest:
            for a in range(3):
                if 0 <= row + 1 - a < ROWS:
                    self.left[row + 1 - a][a * self.rest : (a + 1) * self.rest, :] = shifts[self.whole :]

    def act_steps(self):
        return [lambda r=r: self.store(r) for r in range(ROWS)]

    def conv_steps(self, weight):
        norm = Norm(self.channels // GROUPS)
        source, target = self.hidden, self.hidden_next

        def tap_row(r):
            return self.taps[r][...] if 0 <= r < ROWS else jnp.zeros((self.whole, LANES), BF16)

        def step(k):
            first = k * STEP
            taps = [
                jnp.concatenate([tap_row(first + i + a - 1) for i in range(STEP)], axis=1) for a in range(3)
            ]
            if self.rest:
                taps.append(jnp.concatenate([self.left[first + i][...] for i in range(STEP)], axis=1))
            chunk = source[k][...] + jnp.dot(
                weight(), jnp.concatenate(taps, axis=0), preferred_element_type=F32
            )
            target[k][...] = chunk
            norm.add(chunk)
            if k == len(source) - 1:
                self.scales = norm.scales()
                self.hidden, self.hidden_next = target, source

        return [lambda k=k: step(k) for k in range(len(source))]


class SplitPatch:
    taps_order = [(a, b) for a in range(3) for b in range(3)]

    def __init__(self, hidden, taps, size):
        self.hidden, self.taps, self.size = hidden, taps, size
        self.part = hidden[0][0].shape[0]
        self.scales = [None, None]

    def columns(self, p):
        return slice(p * self.part, (p + 1) * self.part)

    def start_steps(self, p, first_rows):
        norm = Norm(self.size)

        def step(k):
            chunk = first_rows(self.columns(p), k * STEP)
            self.hidden[p][k][...] = chunk
            norm.add(chunk)
            if k == ROWS // STEP - 1:
                self.scales[p] = norm.scales()

        return [lambda k=k: step(k) for k in range(ROWS // STEP)]

    def store(self, p, row):
        chunk = silu(self.hidden[p][row // STEP][:, lanes(row % STEP)], self.scales[p])
        for b, piece in enumerate(col_shifts(chunk)):
            self.taps[p][row][self.columns(b), :] = piece.astype(BF16)

    def act_steps(self, p):
        return [lambda r=r: self.store(p, r) for r in range(ROWS)]

    def product(self, weight_ref, outs, taps, k):
        first = k * STEP
        weights, pieces = [], []
        for p, a, b in taps:
            at = ((3 * a + b) * 2 + p) * self.part
            weights.append(weight_ref[outs, at : at + self.part])
            rows = [first + i + a - 1 for i in range(STEP)]
            blank = jnp.zeros((self.part, LANES), BF16)
            pieces.append(
                jnp.concatenate(
                    [self.taps[p][r][self.columns(b), :] if 0 <= r < ROWS else blank for r in rows], axis=1
                )
            )
        return jnp.dot(
            jnp.concatenate(weights, axis=1), jnp.concatenate(pieces, axis=0), preferred_element_type=F32
        )

    def first_steps(self, weight_ref):
        def step(k):
            taps = [(0, a, b) for a, b in self.taps_order[:-1]]
            added = self.product(weight_ref, slice(0, 2 * self.part), taps, k)
            for p in range(2):
                self.hidden[p][k][...] += added[self.columns(p)]

        return [lambda k=k: step(k) for k in range(ROWS // STEP)]

    def last_steps(self, weight_ref, p):
        norm = Norm(self.size)

        def step(k):
            taps = [(1, a, b) for a, b in self.taps_order] + [(0, *self.taps_order[-1])]
            chunk = self.hidden[p][k][...] + self.product(weight_ref, self.columns(p), taps, k)
            self.hidden[p][k][...] = chunk
            norm.add(chunk)
            if k == ROWS // STEP - 1:
                self.scales[p] = norm.scales()

        return [lambda k=k: step(k) for k in range(ROWS // STEP)]


def run(*columns):
    longest = max(len(c) for c in columns)
    done = [0] * len(columns)
    for i in range(1, longest + 1):
        for k, column in enumerate(columns):
            while done[k] * longest < i * len(column):
                column[done[k]]()
                done[k] += 1


def input_taps(rows, out_ref):
    shifted = [col_shifts(row) for row in rows]
    blank = jnp.zeros_like(rows[0])
    if rows[0].shape[0] % 16 == 0:
        shifted = [[piece.astype(BF16) for piece in pieces] for pieces in shifted]
        blank = blank.astype(BF16)
    for i in range(ROWS):
        pieces = []
        for a in range(3):
            pieces.extend(shifted[i + a - 1] if 0 <= i + a - 1 < ROWS else [blank] * 3)
        out_ref[:, lanes(i)] = jnp.concatenate(pieces, axis=0).astype(BF16)


def place():
    tile = lax.axis_index("tile")
    count = lax.axis_size("tile")
    return lax.rem(tile, 2) == 0, tile == 0, tile == count - 1


def prepare_kernel(embed_ref, embed_out):
    embed_out[...] = jnp.broadcast_to(embed_ref[...], embed_out.shape[::-1]).T


def six_rows_kernel(coarse_ref, pair_ref, mine_ref):
    even, first, last = place()
    sample = lax.axis_index("segment")
    own, pair = ([ref[sample].astype(F32)[:, r, :] for r in range(BAND)] for ref in (coarse_ref, pair_ref))
    for i, (low, high) in enumerate(zip(own + pair[:MARGIN], pair[MARGIN:] + own)):
        mine_ref[:, lanes(i)] = jnp.where(even, low, high).astype(BF16)


def weights_kernel(
    embed_ref, reg_in_ref, reg_mid_ref, diff_in_ref, diff_skip_ref,
    reg_in_out, reg_mid_out, diff_in_out, diff_skip_out,
):
    for source, target in (
        (reg_in_ref, reg_in_out), (diff_in_ref, diff_in_out), (diff_skip_ref, diff_skip_out)
    ):
        target[...] = source[...].astype(F32).T.astype(BF16)
    for block in range(reg_mid_ref.shape[0]):
        reg_mid_out[block] = packed(reg_mid_ref[block])


def coarse_window(mine_ref, across_ref):
    even, first, last = place()
    alone = jnp.logical_or(jnp.logical_and(even, first), jnp.logical_and(jnp.logical_not(even), last))
    mine, across = (
        [ref[:, lanes(i)].astype(F32) for i in range(BAND + MARGIN)] for ref in (mine_ref, across_ref)
    )
    across = [jnp.where(alone, jnp.zeros_like(r), r) for r in across]
    return even, [jnp.where(even, a, b) for a, b in zip(across + mine, mine + across)]


def own_rows(even, window):
    return [jnp.where(even, window[i + BAND], window[i]) for i in range(ROWS)]


def regress_kernel(
    mine_ref, across_ref, reg_in_ref, reg_mid_ref, reg_out_ref,
    rows_ref, skip_ref, reg_ref, send_ref, *refs,
):
    taps_in_a, taps_in_b = refs[-2:]
    even, window = coarse_window(mine_ref, across_ref)
    rows_a = own_rows(even, window)
    rows_b = [jnp.where(even, window[i], window[i + BAND]) for i in range(ROWS)]
    for r in range(ROWS):
        rows_ref[:, lanes(r)] = rows_a[r]
    half = ROWS // STEP
    hidden_out, taps_out, left_out = refs[:half], refs[half : half + ROWS], refs[half + ROWS : half + 2 * ROWS]
    refs = refs[half + 2 * ROWS : -2]
    spare, refs = refs[:half], refs[half:]
    blocks = reg_mid_ref.shape[0]
    hidden_b = (spare, hidden_out) if blocks % 2 == 0 else (hidden_out, spare)
    outer = Patch(*hidden_b, taps_out, left_out)
    own = Patch(refs[:half], refs[half : 2 * half], refs[2 * half : 2 * half + ROWS], refs[2 * half + ROWS :])
    reg_in = reg_in_ref[...]

    def in_steps(patch, rows, taps_in):
        steps = patch.start_steps(
            lambda r: jnp.dot(reg_in, taps_in[:, lanes(r, STEP)], preferred_element_type=F32)
        )
        return [lambda: input_taps(rows, taps_in)] + steps + patch.act_steps()

    run(in_steps(own, rows_a, taps_in_a))
    outer_steps = in_steps(outer, rows_b, taps_in_b)
    for block in range(blocks):
        def weight():
            return reg_mid_ref[block]

        run(own.conv_steps(weight), outer_steps)
        if block < blocks - 1:
            run(outer.conv_steps(weight), own.act_steps())
            outer_steps = outer.act_steps()

    for i in range(BAND):
        skip_ref[:, lanes(i)] = own.rows(MARGIN + i).astype(BF16)
    width = skip_ref.shape[0]
    for i in range(MARGIN):
        send_ref[:width, lanes(i)] = jnp.where(even, own.rows(4 + i), own.rows(2 + i)).astype(BF16)
    reg = []
    for hidden in own.hidden:
        act = silu(hidden[...], [jnp.concatenate([s] * STEP, axis=1) for s in own.scales]).astype(BF16)
        reg.append(jnp.dot(reg_out_ref[...], act, preferred_element_type=F32))
    for k, part in enumerate(reg):
        reg_ref[:, lanes(k * STEP, STEP)] = part
    parts = [jnp.where(even, reg[half // 2 + k], reg[k]) for k in range(half // 2)]
    parts = [part[:, lanes(i, MARGIN)] for part in parts for i in range(0, STEP, MARGIN)]
    tops = [part.astype(BF16).astype(F32) for part in parts]
    parts = tops + [part - top for part, top in zip(parts, tops)]
    send_ref[width:, :] = jnp.concatenate(parts, axis=0).astype(BF16)


def outer_kernel(reg_mid_ref, reg_out_ref, *refs):
    even, first, last = place()
    half = ROWS // STEP
    outer_skip_ref, outer_reg_ref = refs[half + 2 * ROWS : half + 2 * ROWS + 2]
    outer = Patch(
        refs[:half], refs[half + 2 * ROWS + 2 :], refs[half : half + ROWS], refs[half + ROWS : half + 2 * ROWS]
    )
    block = reg_mid_ref.shape[0] - 1
    run(outer.conv_steps(lambda: reg_mid_ref[block]))
    for i in range(MARGIN):
        outer_skip_ref[:, lanes(i)] = jnp.where(even, outer.rows(4 + i), outer.rows(2 + i)).astype(BF16)
    scales = [jnp.concatenate([s] * STEP, axis=1) for s in outer.scales]
    for k in range(half // 2):
        rows = jnp.where(even, outer.hidden[half // 2 + k][...], outer.hidden[k][...])
        outer_reg_ref[:, lanes(k * STEP, STEP)] = jnp.dot(
            reg_out_ref[...], silu(rows, scales).astype(BF16), preferred_element_type=F32
        )


def denoise_kernel(
    rows_ref, noise_ref, skip_ref, reg_ref, pair_ref,
    outer_skip_ref, outer_reg_ref, diff_in_ref, diff_skip_ref, diff_mid_ref, diff_out_ref, embed_ref,
    mean_ref, band_ref, send_pair_ref, send_next_ref,
    taps_in, skips, base, *refs,
):
    even, first, last = place()
    coarse = [rows_ref[:, lanes(r)] for r in range(ROWS)]
    reg = [reg_ref[:, lanes(r)] for r in range(ROWS)]
    width, fields = skip_ref.shape[0], reg_ref.shape[0]
    parts = pair_ref[width:, :].astype(F32)
    parts = parts[: 2 * fields] + parts[2 * fields :]
    pair_reg = [parts[fields * (i // MARGIN) : fields * (i // MARGIN + 1), lanes(i % MARGIN)] for i in range(BAND)]
    up = [jnp.where(even, outer_reg_ref[:, lanes(i)], pair_reg[i]) for i in range(4)]
    down = [jnp.where(even, pair_reg[i], outer_reg_ref[:, lanes(i)]) for i in range(4)]
    mean = []
    for r in range(ROWS):
        both = 0.5 * (reg[r] + (up[r] if r < 4 else down[r - 4]))
        if r < MARGIN:
            mean.append(jnp.where(first, jnp.zeros_like(both), both))
        elif r < 4:
            mean.append(jnp.where(first, reg[r], both))
        elif r < MARGIN + BAND:
            mean.append(jnp.where(last, reg[r], both))
        else:
            mean.append(jnp.where(last, jnp.zeros_like(both), both))
    for i in range(BAND):
        mean_ref[:, lanes(i)] = mean[MARGIN + i]
    mean = [m.astype(BF16).astype(F32) for m in mean]
    for i in range(2):
        low = jnp.where(even, outer_skip_ref[:, lanes(i)], pair_ref[:width, lanes(i)])
        high = jnp.where(even, pair_ref[:width, lanes(i)], outer_skip_ref[:, lanes(i)])
        skips[:, lanes(i)] = jnp.where(first, jnp.zeros_like(low), low)
        skips[:, lanes(6 + i)] = jnp.where(last, jnp.zeros_like(high), high)
    skips[:, lanes(MARGIN, BAND)] = skip_ref[...]
    embed = embed_ref[...]
    noise = noise_ref[lax.axis_index("segment")]
    initial = [sigma_high * noise[:, r, :] for r in range(ROWS)]
    half = ROWS // STEP
    patch = SplitPatch(
        (refs[:half], refs[half : 2 * half]),
        (refs[2 * half : 2 * half + ROWS], refs[2 * half + ROWS :]),
        diff_mid_ref.shape[0] // GROUPS,
    )

    def denoise(current, sigma_now):
        total_var = sigma_now * sigma_now + sigma_data * sigma_data
        input_scale = 1.0 / math.sqrt(total_var)
        skip_coef = sigma_data * sigma_data / total_var
        out_coef = sigma_now * sigma_data / math.sqrt(total_var)
        input_taps(
            [
                jnp.concatenate([input_scale * current[r], coarse[r], mean[r]], axis=0)
                for r in range(ROWS)
            ],
            taps_in,
        )
        shift = jnp.concatenate([(math.log(sigma_now) / 4.0) * embed] * STEP, axis=1)

        def first_rows(outs, r):
            if sigma_now == sigma_high:
                base[outs, lanes(r, STEP)] = jnp.dot(
                    diff_skip_ref[outs, :], skips[:, lanes(r, STEP)], preferred_element_type=F32
                )
            fresh = jnp.dot(diff_in_ref[outs, :], taps_in[:, lanes(r, STEP)], preferred_element_type=F32)
            return fresh + base[outs, lanes(r, STEP)] + shift[outs]

        run(patch.start_steps(0, first_rows))
        run(patch.act_steps(0), patch.start_steps(1, first_rows))
        acts = patch.act_steps(1)
        for k, step in enumerate(patch.first_steps(diff_mid_ref)):
            run(acts[k * STEP : (k + 1) * STEP])
            step()
        run(patch.last_steps(diff_mid_ref, 0))
        run(patch.last_steps(diff_mid_ref, 1))
        scales = [[jnp.concatenate([s] * STEP, axis=1) for s in part] for part in patch.scales]
        acts = []
        for k in range(half):
            pieces = [silu(patch.hidden[p][k][...], scales[p]).astype(BF16) for p in range(2)]
            acts.append(jnp.concatenate(pieces, axis=0))
        outs = jnp.dot(diff_out_ref[...], jnp.concatenate(acts, axis=1), preferred_element_type=F32)
        result = [skip_coef * current[r] + out_coef * outs[:, lanes(r)] for r in range(ROWS)]
        return result

    denoised = denoise(initial, sigma_high)
    stepped = [
        x + (sigma_low - sigma_high) * (x - d) / sigma_high for x, d in zip(initial, denoised)
    ]
    final = denoise(stepped, sigma_low)
    for i in range(BAND):
        band_ref[:, lanes(i)] = final[MARGIN + i]
    for i in range(MARGIN):
        send_pair_ref[:, lanes(i)] = jnp.where(even, final[6 + i], final[i])
        send_next_ref[:, lanes(i)] = jnp.where(even, final[i], final[6 + i])


def pair_average_kernel(band_ref, pair_ref, part_ref):
    even, first, last = place()
    for i in range(BAND):
        here = band_ref[:, lanes(i)]
        both = 0.5 * (here + pair_ref[:, lanes(i % MARGIN)])
        part_ref[:, lanes(i)] = jnp.where(even if i >= MARGIN else jnp.logical_not(even), both, here)


def average_kernel(mean_ref, part_ref, next_ref, own_ref, send_ref):
    even, first, last = place()
    lower = lax.axis_index("segment") == 0
    for i in range(BAND):
        here = part_ref[:, lanes(i)]
        mean = mean_ref[:, lanes(i)]
        both = 0.5 * (here + next_ref[:, lanes(i % MARGIN)])
        done, ends = (jnp.logical_not(even), first) if i < MARGIN else (even, last)
        value = jnp.where(jnp.logical_or(done, ends), here, both) + mean.astype(BF16).astype(F32)
        own_ref[:, i, :] = jnp.where(lower, mean, value)
        send_ref[:, i, :] = jnp.where(lower, value, mean)


def output_kernel(own_ref, got_ref, out_ref):
    lower = lax.axis_index("segment") == 0
    own, got = own_ref[...], got_ref[...]
    out_ref[0, 0] = jnp.where(lower, own, got)
    out_ref[0, 1] = jnp.where(lower, got, own)


def scratch(buffers):
    return [pltpu.VMEM(shape, dtype) for shape, dtype in buffers]


def call(kernel, name, outs, scratch_shapes=(), flops=0):
    return pl.pallas_call(
        kernel,
        name=name,
        out_shape=[jax.ShapeDtypeStruct(shape, dtype) for shape, dtype in outs],
        scratch_shapes=scratch_shapes,
        compiler_params=pltpu.CompilerParams(vmem_limit_bytes=24 * 1024 * 1024),
        cost_estimate=pl.CostEstimate(flops=flops, bytes_accessed=0, transcendentals=0),
    )


def shards(
    coarse, noise_draw, reg_in, reg_mid, reg_out, diff_in, diff_skip, diff_mid, diff_out, noise_embed
):
    tiles, segments = lax.axis_size("tile"), lax.axis_size("segment")
    grid = [(s, t) for s in range(segments) for t in range(tiles)]

    def permute(value, target):
        edges = [(s * tiles + t, target(s, t)[0] * tiles + target(s, t)[1]) for s, t in grid]
        return lax.ppermute(value, ("segment", "tile"), edges)

    def pair(s, t):
        return s, t ^ 1

    def across(s, t):
        to = t - 1 if t % 2 == 0 else t + 1
        return (s, to) if 0 <= to < tiles else ((s + 1) % segments, t)

    def other(s, t):
        return (s + 1) % segments, t

    width_r, width_d, fields, inputs = reg_in.shape[0], diff_in.shape[0], reg_out.shape[0], coarse.shape[1]
    cells, band_cells, edge_cells = ROWS * LANES, BAND * LANES, MARGIN * LANES
    taps_cells = cells + 2 * LANES

    pair_coarse = permute(coarse, pair)
    (embed,) = call(prepare_kernel, "prepare", [((width_d, LANES), F32)], flops=4 * 10**9)(noise_embed[None])
    (mine,) = call(six_rows_kernel, "six_rows", [((inputs, band_cells + edge_cells), BF16)])(
        coarse, pair_coarse
    )
    next_coarse = permute(mine, across)
    reg_in, reg_mid, diff_in, diff_skip = call(
        weights_kernel,
        "weights",
        [(w.shape, BF16) for w in (reg_in, reg_mid, diff_in, diff_skip)],
        flops=4 * 10**9,
    )(embed, reg_in.T, reg_mid, diff_in.T, diff_skip.T)
    hidden_r, taps_r, left_r = patch_shapes(width_r)
    hidden_d = [((width_d // 2, STEP * LANES), F32)] * (2 * ROWS // STEP)
    taps_d = [((3 * width_d // 2, LANES), BF16)] * (2 * ROWS)
    rows, skip, reg, send, *outer = call(
        regress_kernel,
        "regress",
        [
            ((inputs, cells), F32),
            ((width_r, band_cells), BF16),
            ((fields, cells), F32),
            ((width_r + 2 * fields * BAND // MARGIN, edge_cells), BF16),
        ]
        + hidden_r + taps_r + left_r,
        scratch(hidden_r * 3 + taps_r + left_r + [((reg_in.shape[1], cells), BF16)] * 2),
        flops=3 * 10**9,
    )(mine, next_coarse, reg_in, reg_mid, reg_out)
    from_pair = permute(send, pair)
    outer_skip, outer_reg = call(
        outer_kernel,
        "outer",
        [((width_r, edge_cells), BF16), ((fields, band_cells), F32)],
        scratch(hidden_r),
        flops=10**9,
    )(reg_mid, reg_out, *outer)
    mean, band, send_pair, send_next = call(
        denoise_kernel,
        "denoise",
        [
            ((fields, band_cells), F32),
            ((fields, band_cells), F32),
            ((fields, edge_cells), F32),
            ((fields, edge_cells), F32),
        ],
        scratch(
            [((diff_in.shape[1], cells), BF16), ((width_r, cells), BF16), ((width_d, cells), F32)]
            + hidden_d + taps_d
        ),
        flops=4 * 10**9,
    )(
        rows, noise_draw, skip, reg, from_pair,
        outer_skip, outer_reg, diff_in, diff_skip, diff_mid, diff_out, embed,
    )
    pair_band = permute(send_pair, pair)
    next_band = permute(send_next, across)
    piece = ((fields, BAND, LANES), F32)
    (part,) = call(pair_average_kernel, "pair_average", [((fields, band_cells), F32)], flops=2 * 10**9)(
        band, pair_band
    )
    own, send = call(average_kernel, "average", [piece, piece])(mean, part, next_band)
    got = permute(send, other)
    (out,) = call(output_kernel, "output", [((1, 2, fields, BAND, LANES), F32)])(own, got)
    return out


def solution(mesh):
    return jax.shard_map(
        shards,
        mesh=mesh,
        in_specs=(P(None, None, "tile", None), P(None, None, "tile", None)) + (P(),) * 8,
        out_specs=P("segment", None, None, "tile", None),
        check_vma=False,
    )
```
